32 devices in a mesh: cast: 8 (over z, x), width: 4 (over y, core).
Axes of the slice: x: 2, y: 2, z: 4, core: 2. Of those that a mesh axis runs over, the one named last changes fastest.
Arguments:
- stored_caloric_content: float32 [64, 64, 512], P(None, 'cast', 'width'), may hold values from -6 to 6
- zones: int32 [2, 64, 512], P(None, 'cast', 'width'), may hold values from 0 to 9
- spray_coef: float32 [10], replicated, may hold values from 0.2 to 5
Outputs:
- new_enthalpy: float32 [64, 64, 512], P(None, 'cast', 'width')
The draws below stay inside these ranges and needn't reach their ends.
All inputs are finite; a program needn't handle non-finite values.
Results may differ from the reference program's by a relative error of at most 0.0018.
Values sent between devices are 32-bit elements; how exact they have to be, the bound alone decides.
A program may use at most 64 MiB of HBM per device.

```python
import math
import jax
import jax.numpy as jnp
from jax import lax

CX = 8
CY = 128
CZ = 64
ZONES = 10
NX = 64
NY = 512


def draw_stored_caloric_content(key, part):
    key_noise = jax.random.fold_in(key, 0)
    noise_field = jnp.clip(jax.random.normal(key_noise, (CZ, NX, NY), jnp.float32), -4.0, 4.0)
    return noise_field


def draw_zones(key, part):
    key_cast, key_width, key_stray, key_pick = jax.random.split(key, 4)
    offset_cast = jax.random.randint(key_cast, (), 0, NX)
    offset_width = jax.random.randint(key_width, (2, 1, 1), 0, NY)
    cast_place = (jnp.arange(NX, dtype=jnp.int32)[None, :, None] + offset_cast) % NX
    width_place = (jnp.arange(NY, dtype=jnp.int32)[None, None, :] + offset_width) % NY
    segment = cast_place * (ZONES // 2) // NX
    side_half = width_place * 2 // NY
    layout = segment * 2 + side_half
    stray_mask = jax.random.randint(key_stray, (2, NX, NY), 0, 8) == 0
    random_zone = jax.random.randint(key_pick, (2, NX, NY), 0, ZONES)
    return jnp.where(stray_mask, random_zone, layout).astype(jnp.int32)


def setup_inputs(seed: int = 0) -> dict:
    keys = jax.random.split(jax.random.key(seed), 4)
    stored_caloric_content = draw_stored_caloric_content(jax.random.fold_in(keys[3], 71), 0)
    zones = draw_zones(jax.random.fold_in(keys[3], 71), 0)
    spray_coef = jnp.clip(jnp.exp(jax.random.uniform(keys[2], (ZONES,), jnp.float32, math.log(0.2), math.log(5.0))), 0.2, 5.0)
    return dict(stored_caloric_content=stored_caloric_content, zones=zones, spray_coef=spray_coef)


solidification_release = 0.4
quench_medium_hotness = -2.0


def medium_parameters(caloric_content_mesh):
    phase_change_threshold = jnp.tanh(caloric_content_mesh)
    hotness_mesh = caloric_content_mesh - solidification_release * phase_change_threshold
    transport_modulus = 1.5 - 0.5 * jnp.tanh(hotness_mesh)
    caloric_content_incline = (1.0 - solidification_release) + solidification_release * phase_change_threshold * phase_change_threshold
    return hotness_mesh, transport_modulus, caloric_content_incline


def face_pair(cond_first, gain):
    middle_faces = gain * 0.5 * (cond_first[1:] + cond_first[:-1])
    zero_face = jnp.zeros_like(cond_first[:1])
    return jnp.concatenate([zero_face, middle_faces], 0), jnp.concatenate([middle_faces, zero_face], 0)


def displaced_entries_list(caloric_content_mesh):
    before = jnp.concatenate([caloric_content_mesh[:1], caloric_content_mesh[:-1]], 0)
    after = jnp.concatenate([caloric_content_mesh[1:], caloric_content_mesh[-1:]], 0)
    return before, after


def thomas(lower, middle, upper, source):
    zeros_line = jnp.zeros(lower.shape[1:], lower.dtype)

    def forward(carry, row_vals):
        cprime, dprime = carry
        lower_row, middle_row, upper_row, source_row = row_vals
        pivot = middle_row - lower_row * cprime
        new_c = upper_row / pivot
        new_d = (source_row - lower_row * dprime) / pivot
        return (new_c, new_d), (new_c, new_d)

    _, (cprimes, dprimes) = lax.scan(forward, (zeros_line, zeros_line), (lower, middle, upper, source))

    def backward(after_val, row_vals):
        cprime, dprime = row_vals
        value = dprime - cprime * after_val
        return value, value

    _, values = lax.scan(backward, zeros_line, (cprimes, dprimes), reverse=True)
    return values


def line_solve(rhs, transport_modulus, caloric_content_incline, exchange_rim_relation, storage_index_order, gain):
    cond_first = jnp.moveaxis(transport_modulus, storage_index_order, 0)
    slope_first = jnp.moveaxis(caloric_content_incline, storage_index_order, 0)
    bottom_surface_exchange, top_surface_exchange = face_pair(cond_first, gain)
    slope_before, slope_after = displaced_entries_list(slope_first)
    lower = -bottom_surface_exchange * slope_before
    upper = -top_surface_exchange * slope_after
    if storage_index_order == 0:
        middle = 1.0 + slope_first * (bottom_surface_exchange + top_surface_exchange + exchange_rim_relation)
    else:
        middle = 1.0 + slope_first * (bottom_surface_exchange + top_surface_exchange)
    shape_first = lower.shape
    flat_rows = shape_first[0]
    solved = thomas(lower.reshape(flat_rows, -1), middle.reshape(flat_rows, -1), upper.reshape(flat_rows, -1),
                    jnp.moveaxis(rhs, storage_index_order, 0).reshape(flat_rows, -1))
    return jnp.moveaxis(solved.reshape(shape_first), 0, storage_index_order)


def reference(stored_caloric_content, zones, spray_coef):
    hotness_mesh, transport_modulus, caloric_content_incline = medium_parameters(stored_caloric_content)
    surface = spray_coef[zones] * (CZ * CZ / 8.0)
    inner_zero = jnp.zeros((CZ - 2, NX, NY), jnp.float32)
    exchange_rim_relation = jnp.concatenate([surface[0:1], inner_zero, surface[1:2]], 0)
    gains = [(1, CX * CX * 4.0), (2, CY * CY / 4.0), (0, CZ * CZ / 4.0)]
    known_side_increment = exchange_rim_relation * (quench_medium_hotness - hotness_mesh)
    for storage_index_order, gain in gains:
        cond_first = jnp.moveaxis(transport_modulus, storage_index_order, 0)
        hotness_leading_sweep = jnp.moveaxis(hotness_mesh, storage_index_order, 0)
        bottom_surface_exchange, top_surface_exchange = face_pair(cond_first, gain)
        hotness_earlier_step, hotness_later_step = displaced_entries_list(hotness_leading_sweep)
        transport_stream = top_surface_exchange * (hotness_later_step - hotness_leading_sweep) - bottom_surface_exchange * (hotness_leading_sweep - hotness_earlier_step)
        known_side_increment = known_side_increment + jnp.moveaxis(transport_stream, 0, storage_index_order)
    increment = known_side_increment
    for storage_index_order, gain in gains:
        increment = line_solve(increment, transport_modulus, caloric_content_incline, exchange_rim_relation, storage_index_order, gain)
    return stored_caloric_content + increment
```

```python
import functools

import jax
import jax.numpy as jnp
from jax import lax
from jax.experimental import pallas as pl
from jax.experimental.pallas import tpu as pltpu
from jax.sharding import PartitionSpec as P

RELEASE = 0.4
MEDIUM = -2.0


def medium(x):
    t = jnp.tanh(x)
    hot = x - RELEASE * t
    cond = 1.5 - 0.5 * jnp.tanh(hot)
    return t, hot, cond


def level(s, left, right, gl, gr, step, axis):
    size = s.shape[axis]

    def down(a):
        return pltpu.roll(a, step, axis)

    def up(a):
        return pltpu.roll(a, size - step, axis)

    w = 1.0 / (s + left + right + gl + gr)
    al = gl * down(w)
    ga = gr * up(w)
    s2 = s + al * down(s) + ga * up(s)
    left2 = left + al * down(left) + ga * up(left)
    right2 = right + al * down(right) + ga * up(right)
    return s2, left2, right2, al * down(gl), ga * up(gr), al, ga


def apply_level(r, al, ga, step, axis):
    size = r.shape[axis]
    return r + al * pltpu.roll(r, step, axis) + ga * pltpu.roll(r, size - step, axis)


def chain_coefs(a1, a2, b1, b2):
    out = []
    e1 = None
    for i in range(len(a1)):
        if e1 is None:
            c, be = None, None
            f2 = a2[i]
            e1 = b2[i]
        else:
            c = 1.0 / (1.0 - a1[i] * e1)
            be = b1[i] * e1
            f2 = c * a2[i]
            e1 = be * f2 + b2[i]
        out.append((c, be, f2, e1))
    return out


def chain_values(a0, b0, a1, b1, coefs):
    n = len(a0)
    f0s, e0s = [], []
    e0 = None
    for i in range(n):
        c, be, f2, e1 = coefs[i]
        if e0 is None:
            f0 = a0[i]
            e0 = b0[i]
        else:
            f0 = c * (a0[i] + a1[i] * e0)
            e0 = b0[i] + b1[i] * e0 + be * f0
        f0s.append(f0)
        e0s.append(e0)
    first, last = [None] * n, [None] * n
    first[n - 1], last[n - 1] = f0s[n - 1], e0s[n - 1]
    for i in range(n - 2, -1, -1):
        _, _, f2, e1 = coefs[i]
        first[i] = f0s[i] + f2 * first[i + 1]
        last[i] = e0s[i] + e1 * first[i + 1]
    return first, last


def kernel(
    n, nw, x_ref, zones_ref, coef_ref, out_ref,
    T, K, S, Z, U, WL, WR, Y, PP, Q, AL, GA, WW, WP, WQ, D, M, V,
    rows_out, rows_lo, rows_hi, cols_out, cols_lo, cols_hi,
    cs, cr, xs, xr, wc, wv,
    halo_send, halo_recv, a_send, a_recv, b_send, b_recv, c_send, c_recv, d_send, d_recv,
):
    depth, rows, lanes = x_ref.shape
    pz = depth // n
    me = lax.axis_index("cast")
    mw = lax.axis_index("width")
    f32 = jnp.float32

    barrier = pltpu.get_barrier_semaphore()
    for k in range(1, n):
        pl.semaphore_signal(barrier, inc=1, device_id={"cast": lax.rem(me + k, n)})
    for k in range(1, nw):
        pl.semaphore_signal(barrier, inc=1, device_id={"width": lax.rem(mw + k, nw)})

    lane2 = lax.broadcasted_iota(jnp.int32, (rows, lanes), 1)
    row3 = lax.broadcasted_iota(jnp.int32, (pz, rows, lanes), 1)
    lane3 = lax.broadcasted_iota(jnp.int32, (pz, rows, lanes), 2)
    planes3 = lax.broadcasted_iota(jnp.int32, (pz, rows, lanes), 0)
    cast_lo = (me > 0).astype(f32)
    cast_hi = (me < n - 1).astype(f32)
    width_lo = (mw > 0).astype(f32)
    width_hi = (mw < nw - 1).astype(f32)

    def pack(v, b):
        acc = jnp.zeros((rows, lanes), f32)
        for j in range(pz):
            acc = jnp.where(lane2 // 2 == j, pltpu.roll(v[j], 2 * j + 1, 1), acc)
        return pltpu.roll(acc, b * (2 * pz), 1)

    def spread(p, b, odd):
        q = pltpu.roll(p, lax.rem(lanes - b * (2 * pz), lanes), 1)
        return jnp.stack(
            [
                jnp.broadcast_to(q[:, 2 * j + odd : 2 * j + odd + 1], (rows, lanes))
                for j in range(pz)
            ]
        )

    rows_out[0] = x_ref[:, 0, :]
    rows_out[1] = x_ref[:, rows - 1, :]
    cols_out[...] = lax.fori_loop(
        0, n, lambda b, acc: acc + pack(x_ref[pl.ds(b * pz, pz)], b), jnp.zeros((rows, lanes), f32)
    )

    @pl.when(me == 0)
    def _():
        rows_lo[...] = jnp.zeros_like(rows_lo)

    @pl.when(me == n - 1)
    def _():
        rows_hi[...] = jnp.zeros_like(rows_hi)

    @pl.when(mw == 0)
    def _():
        cols_lo[...] = jnp.zeros_like(cols_lo)

    @pl.when(mw == nw - 1)
    def _():
        cols_hi[...] = jnp.zeros_like(cols_hi)

    def remote(src, dst, send, recv, device):
        return pltpu.make_async_remote_copy(
            src_ref=src, dst_ref=dst, send_sem=send, recv_sem=recv,
            device_id=device, device_id_type=pl.DeviceIdType.MESH,
        )

    halos = [
        (remote(rows_out.at[1], rows_lo, halo_send.at[0], halo_recv.at[0],
                {"cast": lax.rem(me + 1, n)}), me < n - 1, me > 0),
        (remote(rows_out.at[0], rows_hi, halo_send.at[1], halo_recv.at[1],
                {"cast": lax.rem(me + n - 1, n)}), me > 0, me < n - 1),
        (remote(cols_out, cols_lo, halo_send.at[2], halo_recv.at[2],
                {"width": lax.rem(mw + 1, nw)}), mw < nw - 1, mw > 0),
        (remote(cols_out, cols_hi, halo_send.at[3], halo_recv.at[3],
                {"width": lax.rem(mw + nw - 1, nw)}), mw > 0, mw < nw - 1),
    ]
    pl.semaphore_wait(barrier, n - 1 + nw - 1)
    for copy, sends, _ in halos:
        pl.when(sends)(copy.start)

    def properties(b, _):
        x = x_ref[pl.ds(b * pz, pz)]
        t, hot, cond = medium(x)
        T[pl.ds(b * pz + 1, pz)] = hot
        K[pl.ds(b * pz + 1, pz)] = cond
        S[pl.ds(b * pz, pz)] = 1.0 / ((1.0 - RELEASE) + RELEASE * t * t)
        U[pl.ds(b * pz, pz)] = jnp.zeros((pz, rows, lanes), f32)
        return 0

    lax.fori_loop(0, n, properties, 0)
    for field in (T, K):
        field[0] = field[1]
        field[depth + 1] = field[depth]
    for side, plane in ((0, 0), (1, depth - 1)):
        zone = zones_ref[side]
        coef = jnp.zeros((rows, lanes), f32)
        for i in range(coef_ref.shape[0]):
            coef = jnp.where(zone == i, coef_ref[i], coef)
        U[plane] = coef * (depth * depth / 8.0)

    for copy, _, receives in halos:
        pl.when(receives)(copy.wait_recv)

    gain_cast = rows * rows * 4.0 * 0.5
    gain_width = lanes * lanes / 4.0 * 0.5
    gain_thick = depth * depth / 4.0 * 0.5
    _, col_lo_T, col_lo_K = medium(cols_lo[...])
    _, col_hi_T, col_hi_K = medium(cols_hi[...])

    def gather_copy(k):
        b = lax.rem(me + n // 2 + k, n)
        return remote(cs.at[b], cr.at[me], a_send.at[k], a_recv.at[k], {"cast": b})

    def cast_block(k, _):
        b = lax.rem(me + n // 2 + k, n)
        z = pl.ds(b * pz, pz)
        hot, cond, s, surf = T[pl.ds(b * pz + 1, pz)], K[pl.ds(b * pz + 1, pz)], S[z], U[z]
        r = surf * (MEDIUM - hot)

        _, hot_n, cond_n = medium(rows_lo[z, :])
        hot_m = jnp.where(row3 == 0, hot_n[:, None, :], pltpu.roll(hot, 1, 1))
        cond_m = jnp.where(row3 == 0, cond_n[:, None, :], pltpu.roll(cond, 1, 1))
        _, hot_n, cond_n = medium(rows_hi[z, :])
        hot_p = jnp.where(row3 == rows - 1, hot_n[:, None, :], pltpu.roll(hot, rows - 1, 1))
        cond_p = jnp.where(row3 == rows - 1, cond_n[:, None, :], pltpu.roll(cond, rows - 1, 1))
        lo = gain_cast * (cond + cond_m) * jnp.where(row3 == 0, cast_lo, 1.0)
        hi = gain_cast * (cond + cond_p) * jnp.where(row3 == rows - 1, cast_hi, 1.0)
        r = r + (hi * (hot_p - hot) - lo * (hot - hot_m))

        hot_m = jnp.where(lane3 == 0, spread(col_lo_T, b, 0), pltpu.roll(hot, 1, 2))
        cond_m = jnp.where(lane3 == 0, spread(col_lo_K, b, 0), pltpu.roll(cond, 1, 2))
        hot_p = jnp.where(lane3 == lanes - 1, spread(col_hi_T, b, 1), pltpu.roll(hot, lanes - 1, 2))
        cond_p = jnp.where(
            lane3 == lanes - 1, spread(col_hi_K, b, 1), pltpu.roll(cond, lanes - 1, 2)
        )
        wlo = gain_width * (cond + cond_m) * jnp.where(lane3 == 0, width_lo, 1.0)
        whi = gain_width * (cond + cond_p) * jnp.where(lane3 == lanes - 1, width_hi, 1.0)
        WL[z] = wlo
        WR[z] = whi
        r = r + (whi * (hot_p - hot) - wlo * (hot - hot_m))

        plane = planes3 + b * pz
        hot_m, cond_m = T[z], K[z]
        hot_p, cond_p = T[pl.ds(b * pz + 2, pz)], K[pl.ds(b * pz + 2, pz)]
        zlo = jnp.where(plane == 0, 0.0, gain_thick * (cond + cond_m))
        zhi = jnp.where(plane == depth - 1, 0.0, gain_thick * (cond + cond_p))
        Z[z] = zlo
        r = r + (zhi * (hot_p - hot) - zlo * (hot - hot_m))

        left = jnp.where(row3 == 0, lo, 0.0)
        right = jnp.where(row3 == rows - 1, hi, 0.0)
        gl, gr = lo - left, hi - right
        step = 1
        while step < rows:
            s, left, right, gl, gr, al, ga = level(s, left, right, gl, gr, step, 1)
            r = apply_level(r, al, ga, step, 1)
            step *= 2
        w = 1.0 / (s + left + right)
        for value, (ref, field) in enumerate(((Y, r * w), (PP, left * w), (Q, right * w))):
            ref[z] = field
            cs[b, value * pz : (value + 1) * pz] = ref[z, 0, :]
            cs[b, (value + 3) * pz : (value + 4) * pz] = ref[z, rows - 1, :]

        @pl.when(b != me)
        def _():
            gather_copy(k).start()

        return 0

    lax.fori_loop(0, n, cast_block, 0)
    cr[me] = cs[me]

    def width_block(b, carry):
        z = pl.ds(b * pz, pz)
        s, lo, hi = S[z], WL[z], WR[z]
        left = jnp.where(lane3 == 0, lo, 0.0)
        right = jnp.where(lane3 == lanes - 1, hi, 0.0)
        gl, gr = lo - left, hi - right
        step, i = 1, 0
        while step < lanes:
            s, left, right, gl, gr, al, ga = level(s, left, right, gl, gr, step, 2)
            AL[i, z] = al
            GA[i, z] = ga
            step, i = step * 2, i + 1
        w = 1.0 / (s + left + right)
        p, q = left * w, right * w
        WW[z], WP[z], WQ[z] = w, p, q
        return carry[0] + pack(p, b), carry[1] + pack(q, b)

    zero = jnp.zeros((rows, lanes), f32)
    p_ends, q_ends = lax.fori_loop(0, n, width_block, (zero, zero))
    wc[mw, 0] = p_ends
    wc[mw, 1] = q_ends
    wide_coefs = [
        remote(wc.at[mw], wc.at[mw], c_send.at[k - 1], c_recv.at[k - 1],
               {"width": lax.rem(mw + k, nw)})
        for k in range(1, nw)
    ]
    for copy in wide_coefs:
        copy.start()

    for k in range(n):
        if k != (n - n // 2) % n:
            gather_copy(k).wait_recv()
    got = [[cr[i, v * pz : (v + 1) * pz] for v in range(6)] for i in range(n)]
    a0, a1, a2, b0, b1, b2 = [[got[i][v] for i in range(n)] for v in range(6)]
    first, last = chain_values(a0, b0, a1, b1, chain_coefs(a1, a2, b1, b2))
    blank = jnp.zeros_like(first[0])

    def answer_copy(i):
        return remote(xs.at[i], xr.at[me], b_send.at[i], b_recv.at[me], {"cast": i})

    for i in range(n):
        xs[i, 0:pz] = last[i - 1] if i > 0 else blank
        xs[i, pz : 2 * pz] = first[i + 1] if i < n - 1 else blank
        pl.when(me != i)(answer_copy(i).start)
    xr[me] = xs[me]

    half = depth // 2
    zlo_sum, zhi_sum = S[0] + U[0], S[depth - 1] + U[depth - 1]
    for i in range(half - 1):
        j = depth - 1 - i
        glo, ghi = Z[i + 1], Z[j]
        wlo, whi = 1.0 / (zlo_sum + glo), 1.0 / (zhi_sum + ghi)
        mlo, mhi = glo * wlo, ghi * whi
        M[i], M[j] = mlo, mhi
        V[i], V[j] = wlo, whi
        zlo_sum = S[i + 1] + mlo * zlo_sum
        zhi_sum = S[j - 1] + mhi * zhi_sum
    gmid = Z[half]
    det = 1.0 / (zlo_sum * zhi_sum + gmid * (zlo_sum + zhi_sum))
    V[half - 1] = (zhi_sum + gmid) * det
    V[half] = (zlo_sum + gmid) * det
    M[half] = gmid * det

    def step_block(k, carry):
        b = lax.rem(me + k, n)

        @pl.when(k > 0)
        def _():
            remote(xs.at[b], xr.at[b], b_send.at[b], b_recv.at[b], {"cast": b}).wait_recv()

        z = pl.ds(b * pz, pz)
        lo, hi = xr[b, 0:pz], xr[b, pz : 2 * pz]
        r = (Y[z] + PP[z] * lo[:, None, :] + Q[z] * hi[:, None, :]) * S[z]
        step, i = 1, 0
        while step < lanes:
            r = apply_level(r, AL[i, z], GA[i, z], step, 2)
            step, i = step * 2, i + 1
        r = r * WW[z]
        D[z] = r
        return carry + pack(r, b)

    wv[mw] = lax.fori_loop(0, n, step_block, zero)
    wide_values = [
        remote(wv.at[mw], wv.at[mw], d_send.at[k - 1], d_recv.at[k - 1],
               {"width": lax.rem(mw + k, nw)})
        for k in range(1, nw)
    ]
    for copy in wide_values:
        copy.start()

    for copy in wide_coefs:
        copy.wait_recv()

    def firsts(p):
        return pltpu.roll(p, lanes - 1, 1)

    even = lane2 % 2 == 0
    b1 = [jnp.where(even, wc[i, 0], 0.0) for i in range(nw)]
    b2 = [jnp.where(even, wc[i, 1], 0.0) for i in range(nw)]
    a1 = [jnp.where(even, firsts(wc[i, 0]), 0.0) for i in range(nw)]
    a2 = [jnp.where(even, firsts(wc[i, 1]), 0.0) for i in range(nw)]
    coefs = chain_coefs(a1, a2, b1, b2)
    for copy in wide_values:
        copy.wait_recv()
    b0 = [wv[i] for i in range(nw)]
    a0 = [firsts(b0[i]) for i in range(nw)]
    first, last = chain_values(a0, b0, a1, b1, coefs)
    before, after = zero, zero
    for i in range(nw):
        if i > 0:
            before = jnp.where(mw == i, last[i - 1], before)
        if i < nw - 1:
            after = jnp.where(mw == i, first[i + 1], after)

    def thick_block(b, _):
        z = pl.ds(b * pz, pz)
        D[z] = (D[z] + WP[z] * spread(before, b, 0) + WQ[z] * spread(after, b, 0)) * S[z]
        return 0

    lax.fori_loop(0, n, thick_block, 0)

    dlo, dhi = D[0], D[depth - 1]
    for i in range(half - 1):
        j = depth - 1 - i
        D[i], D[j] = dlo, dhi
        dlo = D[i + 1] + M[i] * dlo
        dhi = D[j - 1] + M[j] * dhi
    ulo = V[half - 1] * dlo + M[half] * dhi
    uhi = V[half] * dhi + M[half] * dlo
    out_ref[half - 1] = ulo * S[half - 1]
    out_ref[half] = uhi * S[half]
    for i in range(half - 2, -1, -1):
        j = depth - 1 - i
        ulo = V[i] * D[i] + M[i] * ulo
        uhi = V[j] * D[j] + M[j] * uhi
        out_ref[i] = ulo * S[i]
        out_ref[j] = uhi * S[j]

    for copy, sends, _ in halos:
        pl.when(sends)(copy.wait_send)
    for k in range(n):
        if k != (n - n // 2) % n:
            gather_copy(k).wait_send()
    for i in range(n):
        pl.when(me != i)(answer_copy(i).wait_send)
    for copy in wide_coefs + wide_values:
        copy.wait_send()


def shards(n, nw, x, zones, spray_coef):
    depth, rows, lanes = x.shape
    pz = depth // n
    f32 = jnp.float32
    vmem = pltpu.VMEM
    field = vmem((depth, rows, lanes), f32)
    padded = vmem((depth + 2, rows, lanes), f32)
    levels = vmem(((lanes - 1).bit_length(), depth, rows, lanes), f32)
    edge = vmem((depth, lanes), f32)
    packed = vmem((rows, lanes), f32)
    dma = pltpu.SemaphoreType.DMA
    scratch = (
        [padded, padded]
        + [field] * 8
        + [levels, levels]
        + [field] * 6
        + [vmem((2, depth, lanes), f32), edge, edge, packed, packed, packed]
        + [
            vmem((n, 6 * pz, lanes), f32),
            vmem((n, 6 * pz, lanes), f32),
            vmem((n, 2 * pz, lanes), f32),
            vmem((n, 2 * pz, lanes), f32),
            vmem((nw, 2, rows, lanes), f32),
            vmem((nw, rows, lanes), f32),
        ]
        + [dma((4,)), dma((4,))]
        + [dma((n,))] * 4
        + [dma((nw,))] * 4
    )
    step = pl.pallas_call(
        functools.partial(kernel, n, nw),
        out_shape=jax.ShapeDtypeStruct(x.shape, f32),
        in_specs=[
            pl.BlockSpec(memory_space=pltpu.VMEM),
            pl.BlockSpec(memory_space=pltpu.VMEM),
            pl.BlockSpec(memory_space=pltpu.SMEM),
        ],
        out_specs=pl.BlockSpec(memory_space=pltpu.VMEM),
        scratch_shapes=scratch,
        compiler_params=pltpu.CompilerParams(
            collective_id=0, has_side_effects=True, vmem_limit_bytes=32 * 1024 * 1024
        ),
        cost_estimate=pl.CostEstimate(
            flops=20_000_000, bytes_accessed=1_000_000, transcendentals=100_000
        ),
        name="adi_step",
    )(x, zones, spray_coef)
    return x + step


def solution(mesh):
    spec = P(None, "cast", "width")
    body = functools.partial(shards, mesh.shape["cast"], mesh.shape["width"])
    return jax.shard_map(
        body, mesh=mesh, in_specs=(spec, spec, P()), out_specs=spec, check_vma=False
    )
```

```python
import functools

import jax
import jax.numpy as jnp
from jax import lax
from jax.experimental import pallas as pl
from jax.experimental.pallas import tpu as pltpu
from jax.sharding import PartitionSpec as P

RELEASE = 0.4
MEDIUM = -2.0


def medium(x):
    t = jnp.tanh(x)
    hot = x - RELEASE * t
    cond = 1.5 - 0.5 * jnp.tanh(hot)
    return t, hot, cond


def lane_levels(ground, gl, gr, left, right):
    axis = ground.ndim - 1
    size = ground.shape[axis]
    lane = lax.broadcasted_iota(jnp.int32, ground.shape, axis)
    ends = left + right
    factors = []
    step = 1
    while step < size:
        w = 1.0 / (ground + gl + gr)
        al = gl * pltpu.roll(w, step, axis)
        ga = gr * pltpu.roll(w, size - step, axis)
        factors.append((al, ga))
        ground = (
            ground
            + al * pltpu.roll(ground, step, axis)
            + ga * pltpu.roll(ground, size - step, axis)
        )
        from_left = al * pltpu.roll(ends, step, axis)
        from_right = ga * pltpu.roll(ends, size - step, axis)
        if 2 * step < size:
            ends = ends + from_left + from_right
            gl = al * pltpu.roll(gl, step, axis)
            gr = ga * pltpu.roll(gr, size - step, axis)
        else:
            left = jnp.where(lane < step, ends, 0.0) + from_left
            right = jnp.where(lane >= step, ends, 0.0) + from_right
        step *= 2
    return ground, left, right, factors


def row_levels(ground, links, left, right, r):
    count = len(ground)
    zero = jnp.zeros_like(left)
    ground = list(ground)
    ground[0] = ground[0] + left
    ground[-1] = ground[-1] + right
    lefts = [left] + [zero] * (count - 1)
    rights = [zero] * (count - 1) + [right]
    step = 1
    while step < count:
        w = []
        for j in range(count):
            total = ground[j]
            if j >= step:
                total = total + links[j - step]
            if j + step < count:
                total = total + links[j]
            w.append(1.0 / total)
        new_ground, new_r = list(ground), list(r)
        new_left, new_right = list(lefts), list(rights)
        new_links = [None] * count
        for j in range(count):
            if j >= step:
                al = links[j - step] * w[j - step]
                new_ground[j] = new_ground[j] + al * ground[j - step]
                new_r[j] = new_r[j] + al * r[j - step]
                if j - step < step:
                    new_left[j] = new_left[j] + al * lefts[j - step]
                if j >= 2 * step:
                    new_links[j - 2 * step] = al * links[j - 2 * step]
            if j + step < count:
                ga = links[j] * w[j + step]
                new_ground[j] = new_ground[j] + ga * ground[j + step]
                new_r[j] = new_r[j] + ga * r[j + step]
                if j + step >= count - step:
                    new_right[j] = new_right[j] + ga * rights[j + step]
        ground, r, lefts, rights, links = new_ground, new_r, new_left, new_right, new_links
        step *= 2
    w = [1.0 / g for g in ground]
    return [[a * b for a, b in zip(v, w)] for v in (r, lefts, rights)]


def apply_level(r, al, ga, step, axis):
    size = r.shape[axis]
    return r + al * pltpu.roll(r, step, axis) + ga * pltpu.roll(r, size - step, axis)


def chain_coefs(a1, a2, b1, b2):
    out = []
    e1 = None
    for i in range(len(a1)):
        if e1 is None:
            c, be = None, None
            f2 = a2[i]
            e1 = b2[i]
        else:
            c = 1.0 / (1.0 - a1[i] * e1)
            be = b1[i] * e1
            f2 = c * a2[i]
            e1 = be * f2 + b2[i]
        out.append((c, be, f2, e1))
    return out


def chain_values(a0, b0, a1, b1, coefs):
    n = len(a0)
    f0s, e0s = [], []
    e0 = None
    for i in range(n):
        c, be, f2, e1 = coefs[i]
        if e0 is None:
            f0 = a0[i]
            e0 = b0[i]
        else:
            f0 = c * (a0[i] + a1[i] * e0)
            e0 = b0[i] + b1[i] * e0 + be * f0
        f0s.append(f0)
        e0s.append(e0)
    first, last = [None] * n, [None] * n
    first[n - 1], last[n - 1] = f0s[n - 1], e0s[n - 1]
    for i in range(n - 2, -1, -1):
        _, _, f2, e1 = coefs[i]
        first[i] = f0s[i] + f2 * first[i + 1]
        last[i] = e0s[i] + e1 * first[i + 1]
    return first, last


def kernel(
    n, nw, x_hbm, zones_hbm, coef_ref, out_ref,
    x_ref, zones_ref, T, K, S, U, SX, WL, WR, Y, PP, Q, AL, GA, WW, WP, WQ, DX, D, M, V,
    rows_out, rows_lo, rows_hi, cols_out, cols_lo, cols_hi,
    cs, cr, xs, xr, wc, wv,
    in_sem, halo_send, halo_recv, a_send, a_recv, b_send, b_recv, c_send, c_recv, d_send, d_recv,
):
    depth, rows, lanes = x_ref.shape
    pz = depth // n
    bz = SX.shape[2]
    nb = depth // bz
    per = bz // pz
    me = lax.axis_index("cast")
    mw = lax.axis_index("width")
    f32 = jnp.float32

    x_copy = pltpu.make_async_copy(x_hbm, x_ref, in_sem.at[0])
    zones_copy = pltpu.make_async_copy(zones_hbm, zones_ref, in_sem.at[1])
    x_copy.start()
    zones_copy.start()

    barrier = pltpu.get_barrier_semaphore()
    for k in range(1, n):
        pl.semaphore_signal(barrier, inc=1, device_id={"cast": lax.rem(me + k, n)})
    for k in range(1, nw):
        pl.semaphore_signal(barrier, inc=1, device_id={"width": lax.rem(mw + k, nw)})

    lane2 = lax.broadcasted_iota(jnp.int32, (bz, lanes), 1)
    lane3 = lax.broadcasted_iota(jnp.int32, (rows, bz, lanes), 2)
    zero = jnp.zeros((bz, lanes), f32)
    cast_lo = (me > 0).astype(f32)
    cast_hi = (me < n - 1).astype(f32)
    width_lo = (mw > 0).astype(f32)
    width_hi = (mw < nw - 1).astype(f32)

    def pack(v, b):
        acc = zero
        for j in range(rows):
            acc = jnp.where(lane2 // 2 == j, pltpu.roll(v[j], 2 * j + 1, 1), acc)
        return pltpu.roll(acc, b * (2 * rows), 1)

    def spread(p, b, odd):
        q = pltpu.roll(p, lax.rem(lanes - b * (2 * rows), lanes), 1)
        return [
            jnp.broadcast_to(q[:, 2 * j + odd : 2 * j + odd + 1], (bz, lanes))
            for j in range(rows)
        ]

    def by_rows(ref, start):
        return [ref[pl.ds(start, bz), j, :] for j in range(rows)]

    x_copy.wait()
    rows_out[0] = x_ref[:, 0, :]
    rows_out[1] = x_ref[:, rows - 1, :]
    cols_out[...] = lax.fori_loop(
        0, nb, lambda b, acc: acc + pack(by_rows(x_ref, b * bz), b), zero
    )

    @pl.when(me == 0)
    def _():
        rows_lo[...] = jnp.zeros_like(rows_lo)

    @pl.when(me == n - 1)
    def _():
        rows_hi[...] = jnp.zeros_like(rows_hi)

    @pl.when(mw == 0)
    def _():
        cols_lo[...] = jnp.zeros_like(cols_lo)

    @pl.when(mw == nw - 1)
    def _():
        cols_hi[...] = jnp.zeros_like(cols_hi)

    def remote(src, dst, send, recv, device):
        return pltpu.make_async_remote_copy(
            src_ref=src, dst_ref=dst, send_sem=send, recv_sem=recv,
            device_id=device, device_id_type=pl.DeviceIdType.MESH,
        )

    halos = [
        (remote(rows_out.at[1], rows_lo, halo_send.at[0], halo_recv.at[0],
                {"cast": lax.rem(me + 1, n)}), me < n - 1, me > 0),
        (remote(rows_out.at[0], rows_hi, halo_send.at[1], halo_recv.at[1],
                {"cast": lax.rem(me + n - 1, n)}), me > 0, me < n - 1),
        (remote(cols_out, cols_lo, halo_send.at[2], halo_recv.at[2],
                {"width": lax.rem(mw + 1, nw)}), mw < nw - 1, mw > 0),
        (remote(cols_out, cols_hi, halo_send.at[3], halo_recv.at[3],
                {"width": lax.rem(mw + nw - 1, nw)}), mw > 0, mw < nw - 1),
    ]
    pl.semaphore_wait(barrier, n - 1 + nw - 1)
    for copy, sends, _ in halos:
        pl.when(sends)(copy.start)

    def properties(b, _):
        z = pl.ds(b * bz, bz)
        t, hot, cond = medium(x_ref[z])
        T[pl.ds(b * bz + 1, bz)] = hot
        K[pl.ds(b * bz + 1, bz)] = cond
        S[z] = 1.0 / ((1.0 - RELEASE) + RELEASE * t * t)
        U[z] = jnp.zeros((bz, rows, lanes), f32)
        for j, v in enumerate(by_rows(S, b * bz)):
            SX[b, j] = v
        return 0

    lax.fori_loop(0, nb, properties, 0)
    T[0], T[depth + 1] = T[1], T[depth]
    K[0], K[depth + 1] = -K[1], -K[depth]
    zones_copy.wait()
    for side, plane in ((0, 0), (1, depth - 1)):
        zone = zones_ref[side]
        coef = jnp.zeros((rows, lanes), f32)
        for i in range(coef_ref.shape[0]):
            coef = jnp.where(zone == i, coef_ref[i], coef)
        U[plane] = coef * (depth * depth / 8.0)

    for copy, _, receives in halos:
        pl.when(receives)(copy.wait_recv)

    gain_cast = rows * rows * 4.0 * 0.5
    gain_width = lanes * lanes / 4.0 * 0.5
    gain_thick = depth * depth / 4.0 * 0.5
    width_lo_mask = jnp.where(lane2 == 0, width_lo, 1.0)
    width_hi_mask = jnp.where(lane2 == lanes - 1, width_hi, 1.0)
    _, col_lo_T, col_lo_K = medium(cols_lo[...])
    _, col_hi_T, col_hi_K = medium(cols_hi[...])

    def gather_copy(dest):
        return remote(cs.at[dest], cr.at[me], a_send.at[dest], a_recv.at[me], {"cast": dest})

    def gather_wait(source):
        remote(cs.at[source], cr.at[source], a_send.at[source], a_recv.at[source],
               {"cast": source}).wait_recv()

    def cast_block(k, _):
        b = lax.rem(me // per + nb // 2 + k, nb)
        start = pl.multiple_of(b * bz, bz)
        hot, cond = by_rows(T, start + 1), by_rows(K, start + 1)
        hot_m, cond_m = by_rows(T, start), by_rows(K, start)
        hot_p, cond_p = by_rows(T, start + 2), by_rows(K, start + 2)
        surf = by_rows(U, start)
        _, hot_lo, cond_lo = medium(rows_lo[pl.ds(start, bz), :])
        _, hot_hi, cond_hi = medium(rows_hi[pl.ds(start, bz), :])
        hots, conds = [hot_lo] + hot + [hot_hi], [cond_lo] + cond + [cond_hi]
        faces = [gain_cast * (conds[j] + conds[j + 1]) for j in range(rows + 1)]
        faces[0], faces[rows] = faces[0] * cast_lo, faces[rows] * cast_hi
        flux = [faces[j] * (hots[j + 1] - hots[j]) for j in range(rows + 1)]

        lo_T, lo_K = spread(col_lo_T, b, 0), spread(col_lo_K, b, 0)
        hi_T, hi_K = spread(col_hi_T, b, 1), spread(col_hi_K, b, 1)
        r = []
        for j in range(rows):
            h, c = hot[j], cond[j]
            hm = jnp.where(lane2 == 0, lo_T[j], pltpu.roll(h, 1, 1))
            cm = jnp.where(lane2 == 0, lo_K[j], pltpu.roll(c, 1, 1))
            hp = jnp.where(lane2 == lanes - 1, hi_T[j], pltpu.roll(h, lanes - 1, 1))
            cp = jnp.where(lane2 == lanes - 1, hi_K[j], pltpu.roll(c, lanes - 1, 1))
            lo = gain_width * (c + cm) * width_lo_mask
            hi = gain_width * (c + cp) * width_hi_mask
            WL[b, j] = lo
            WR[b, j] = hi
            r.append(
                surf[j] * (MEDIUM - h)
                + (flux[j + 1] - flux[j])
                + (hi * (hp - h) - lo * (h - hm))
                + gain_thick
                * ((c + cond_p[j]) * (hot_p[j] - h) - (c + cond_m[j]) * (h - hot_m[j]))
            )
        s = [SX[b, j] for j in range(rows)]
        ys, ps, qs = row_levels(s, faces[1:rows], faces[0], faces[rows], r)
        for j in range(rows):
            Y[b, j] = ys[j]
            PP[b, j] = ps[j]
            Q[b, j] = qs[j]
        for o in range(per):
            dest = b * per + o
            for v, value in enumerate((ys[0], ps[0], qs[0], ys[-1], ps[-1], qs[-1])):
                cs[dest, v * pz : (v + 1) * pz] = value[o * pz : (o + 1) * pz]

            @pl.when(dest != me)
            def _():
                gather_copy(dest).start()

        return 0

    lax.fori_loop(0, nb, cast_block, 0)
    cr[me] = cs[me]

    def width_block(b, carry):
        lo, hi = WL[b], WR[b]
        left = jnp.where(lane3 == 0, lo, 0.0)
        right = jnp.where(lane3 == lanes - 1, hi, 0.0)
        ground, left, right, factors = lane_levels(
            SX[b] + left + right, lo - left, hi - right, left, right
        )
        for i, (al, ga) in enumerate(factors):
            AL[i, b] = al
            GA[i, b] = ga
        w = 1.0 / ground
        p, q = left * w, right * w
        WW[b], WP[b], WQ[b] = w, p, q
        return carry[0] + pack(p, b), carry[1] + pack(q, b)

    p_ends, q_ends = lax.fori_loop(0, nb, width_block, (zero, zero))
    wc[mw, 0] = p_ends
    wc[mw, 1] = q_ends
    wide_coefs = [
        remote(wc.at[mw], wc.at[mw], c_send.at[k - 1], c_recv.at[k - 1],
               {"width": lax.rem(mw + k, nw)})
        for k in range(1, nw)
    ]
    for copy in wide_coefs:
        copy.start()

    for i in range(n):
        pl.when(me != i)(functools.partial(gather_wait, i))
    got = [[cr[i, v * pz : (v + 1) * pz] for v in range(6)] for i in range(n)]
    a0, a1, a2, b0, b1, b2 = [[got[i][v] for i in range(n)] for v in range(6)]
    first, last = chain_values(a0, b0, a1, b1, chain_coefs(a1, a2, b1, b2))
    blank = jnp.zeros_like(first[0])

    def answer_copy(i):
        return remote(xs.at[i], xr.at[me], b_send.at[i], b_recv.at[me], {"cast": i})

    for i in range(n):
        xs[i, 0:pz] = last[i - 1] if i > 0 else blank
        xs[i, pz : 2 * pz] = first[i + 1] if i < n - 1 else blank
        pl.when(me != i)(answer_copy(i).start)
    xr[me] = xs[me]

    half = depth // 2
    zlo_sum, zhi_sum = S[0] + U[0], S[depth - 1] + U[depth - 1]
    for i in range(half - 1):
        j = depth - 1 - i
        glo, ghi = gain_thick * (K[i + 1] + K[i + 2]), gain_thick * (K[j] + K[j + 1])
        wlo, whi = 1.0 / (zlo_sum + glo), 1.0 / (zhi_sum + ghi)
        mlo, mhi = glo * wlo, ghi * whi
        M[i], M[j] = mlo, mhi
        V[i], V[j] = wlo, whi
        zlo_sum = S[i + 1] + mlo * zlo_sum
        zhi_sum = S[j - 1] + mhi * zhi_sum
    gmid = gain_thick * (K[half] + K[half + 1])
    det = 1.0 / (zlo_sum * zhi_sum + gmid * (zlo_sum + zhi_sum))
    V[half - 1] = (zhi_sum + gmid) * det
    V[half] = (zlo_sum + gmid) * det
    M[half] = gmid * det

    def step_block(k, carry):
        b = lax.rem(me // per + k, nb)
        los, his = [], []
        for o in range(per):
            owner = b * per + o

            @pl.when(owner != me)
            def _():
                remote(xs.at[owner], xr.at[owner], b_send.at[owner], b_recv.at[owner],
                       {"cast": owner}).wait_recv()

            los.append(xr[owner, 0:pz])
            his.append(xr[owner, pz : 2 * pz])
        lo = los[0] if per == 1 else jnp.concatenate(los, 0)
        hi = his[0] if per == 1 else jnp.concatenate(his, 0)
        r = (Y[b] + PP[b] * lo[None] + Q[b] * hi[None]) * SX[b]
        step, i = 1, 0
        while step < lanes:
            r = apply_level(r, AL[i, b], GA[i, b], step, 2)
            step, i = step * 2, i + 1
        r = r * WW[b]
        DX[b] = r
        return carry + pack(r, b)

    wv[mw] = lax.fori_loop(0, nb, step_block, zero)
    wide_values = [
        remote(wv.at[mw], wv.at[mw], d_send.at[k - 1], d_recv.at[k - 1],
               {"width": lax.rem(mw + k, nw)})
        for k in range(1, nw)
    ]
    for copy in wide_values:
        copy.start()

    for copy in wide_coefs:
        copy.wait_recv()

    def firsts(p):
        return pltpu.roll(p, lanes - 1, 1)

    even = lane2 % 2 == 0
    b1 = [jnp.where(even, wc[i, 0], 0.0) for i in range(nw)]
    b2 = [jnp.where(even, wc[i, 1], 0.0) for i in range(nw)]
    a1 = [jnp.where(even, firsts(wc[i, 0]), 0.0) for i in range(nw)]
    a2 = [jnp.where(even, firsts(wc[i, 1]), 0.0) for i in range(nw)]
    coefs = chain_coefs(a1, a2, b1, b2)
    for copy in wide_values:
        copy.wait_recv()
    b0 = [wv[i] for i in range(nw)]
    a0 = [firsts(b0[i]) for i in range(nw)]
    first, last = chain_values(a0, b0, a1, b1, coefs)
    before, after = zero, zero
    for i in range(nw):
        if i > 0:
            before = jnp.where(mw == i, last[i - 1], before)
        if i < nw - 1:
            after = jnp.where(mw == i, first[i + 1], after)

    def thick_block(b, _):
        start = b * bz
        los, his = spread(before, b, 0), spread(after, b, 0)
        for j in range(rows):
            D[pl.ds(start, bz), j, :] = (DX[b, j] + WP[b, j] * los[j] + WQ[b, j] * his[j]) * SX[
                b, j
            ]
        return 0

    lax.fori_loop(0, nb, thick_block, 0)

    dlo, dhi = D[0], D[depth - 1]
    for i in range(half - 1):
        j = depth - 1 - i
        D[i], D[j] = dlo, dhi
        dlo = D[i + 1] + M[i] * dlo
        dhi = D[j - 1] + M[j] * dhi
    ulo = V[half - 1] * dlo + M[half] * dhi
    uhi = V[half] * dhi + M[half] * dlo
    out_ref[half - 1] = ulo * S[half - 1]
    out_ref[half] = uhi * S[half]
    for i in range(half - 2, -1, -1):
        j = depth - 1 - i
        ulo = V[i] * D[i] + M[i] * ulo
        uhi = V[j] * D[j] + M[j] * uhi
        out_ref[i] = ulo * S[i]
        out_ref[j] = uhi * S[j]

    for copy, sends, _ in halos:
        pl.when(sends)(copy.wait_send)
    for i in range(n):
        pl.when(me != i)(gather_copy(i).wait_send)
    for i in range(n):
        pl.when(me != i)(answer_copy(i).wait_send)
    for copy in wide_coefs + wide_values:
        copy.wait_send()


def shards(n, nw, x, zones, spray_coef):
    depth, rows, lanes = x.shape
    pz = depth // n
    f32 = jnp.float32
    vmem = pltpu.VMEM
    bz = max(pz, rows)
    nb = depth // bz
    field = vmem((depth, rows, lanes), f32)
    blocks = vmem((nb, rows, bz, lanes), f32)
    padded = vmem((depth + 2, rows, lanes), f32)
    levels = vmem(((lanes - 1).bit_length(), nb, rows, bz, lanes), f32)
    edge = vmem((depth, lanes), f32)
    packed = vmem((bz, lanes), f32)
    dma = pltpu.SemaphoreType.DMA
    scratch = (
        [field, vmem(zones.shape, zones.dtype), padded, padded]
        + [field, field]
        + [blocks] * 6
        + [levels, levels]
        + [blocks] * 4
        + [field] * 3
        + [vmem((2, depth, lanes), f32), edge, edge, packed, packed, packed]
        + [
            vmem((n, 6 * pz, lanes), f32),
            vmem((n, 6 * pz, lanes), f32),
            vmem((n, 2 * pz, lanes), f32),
            vmem((n, 2 * pz, lanes), f32),
            vmem((nw, 2, bz, lanes), f32),
            vmem((nw, bz, lanes), f32),
        ]
        + [dma((2,)), dma((4,)), dma((4,))]
        + [dma((n,))] * 4
        + [dma((nw,))] * 4
    )
    step = pl.pallas_call(
        functools.partial(kernel, n, nw),
        out_shape=jax.ShapeDtypeStruct(x.shape, f32),
        in_specs=[
            pl.BlockSpec(memory_space=pl.ANY),
            pl.BlockSpec(memory_space=pl.ANY),
            pl.BlockSpec(memory_space=pltpu.SMEM),
        ],
        out_specs=pl.BlockSpec(memory_space=pltpu.VMEM),
        scratch_shapes=scratch,
        compiler_params=pltpu.CompilerParams(
            collective_id=0, has_side_effects=True, vmem_limit_bytes=32 * 1024 * 1024
        ),
        cost_estimate=pl.CostEstimate(
            flops=20_000_000, bytes_accessed=1_000_000, transcendentals=100_000
        ),
        name="adi_step",
    )(x, zones, spray_coef)
    return x + step


def solution(mesh):
    spec = P(None, "cast", "width")
    body = functools.partial(shards, mesh.shape["cast"], mesh.shape["width"])
    return jax.shard_map(
        body, mesh=mesh, in_specs=(spec, spec, P()), out_specs=spec, check_vma=False
    )
```

```python
import functools

import jax
import jax.numpy as jnp
from jax import lax
from jax.experimental import pallas as pl
from jax.experimental.pallas import tpu as pltpu
from jax.sharding import PartitionSpec as P

RELEASE = 0.4
MEDIUM = -2.0


def medium(x):
    t = jnp.tanh(x)
    hot = x - RELEASE * t
    cond = 1.5 - 0.5 * jnp.tanh(hot)
    return t, hot, cond


def lane_levels(ground, gl, gr, left, right):
    axis = ground.ndim - 1
    size = ground.shape[axis]
    lane = lax.broadcasted_iota(jnp.int32, ground.shape, axis)
    ends = left + right
    factors = []
    step = 1
    while step < size:
        w = 1.0 / (ground + gl + gr)
        al = gl * pltpu.roll(w, step, axis)
        ga = gr * pltpu.roll(w, size - step, axis)
        factors.append((al, ga))
        ground = (
            ground
            + al * pltpu.roll(ground, step, axis)
            + ga * pltpu.roll(ground, size - step, axis)
        )
        from_left = al * pltpu.roll(ends, step, axis)
        from_right = ga * pltpu.roll(ends, size - step, axis)
        if 2 * step < size:
            ends = ends + from_left + from_right
            gl = al * pltpu.roll(gl, step, axis)
            gr = ga * pltpu.roll(gr, size - step, axis)
        else:
            left = jnp.where(lane < step, ends, 0.0) + from_left
            right = jnp.where(lane >= step, ends, 0.0) + from_right
        step *= 2
    return ground, left, right, factors


def row_levels(ground, links, left, right, r):
    count = len(ground)
    zero = jnp.zeros_like(left)
    ground = list(ground)
    ground[0] = ground[0] + left
    ground[-1] = ground[-1] + right
    lefts = [left] + [zero] * (count - 1)
    rights = [zero] * (count - 1) + [right]
    step = 1
    while step < count:
        w = []
        for j in range(count):
            total = ground[j]
            if j >= step:
                total = total + links[j - step]
            if j + step < count:
                total = total + links[j]
            w.append(1.0 / total)
        new_ground, new_r = list(ground), list(r)
        new_left, new_right = list(lefts), list(rights)
        new_links = [None] * count
        for j in range(count):
            if j >= step:
                al = links[j - step] * w[j - step]
                new_ground[j] = new_ground[j] + al * ground[j - step]
                new_r[j] = new_r[j] + al * r[j - step]
                if j - step < step:
                    new_left[j] = new_left[j] + al * lefts[j - step]
                if j >= 2 * step:
                    new_links[j - 2 * step] = al * links[j - 2 * step]
            if j + step < count:
                ga = links[j] * w[j + step]
                new_ground[j] = new_ground[j] + ga * ground[j + step]
                new_r[j] = new_r[j] + ga * r[j + step]
                if j + step >= count - step:
                    new_right[j] = new_right[j] + ga * rights[j + step]
        ground, r, lefts, rights, links = new_ground, new_r, new_left, new_right, new_links
        step *= 2
    w = [1.0 / g for g in ground]
    return [[a * b for a, b in zip(v, w)] for v in (r, lefts, rights)]


def apply_level(r, al, ga, step, axis):
    size = r.shape[axis]
    return r + al * pltpu.roll(r, step, axis) + ga * pltpu.roll(r, size - step, axis)


def chain_coefs(a1, a2, b1, b2):
    out = []
    e1 = None
    for i in range(len(a1)):
        if e1 is None:
            c, be = None, None
            f2 = a2[i]
            e1 = b2[i]
        else:
            c = 1.0 / (1.0 - a1[i] * e1)
            be = b1[i] * e1
            f2 = c * a2[i]
            e1 = be * f2 + b2[i]
        out.append((c, be, f2, e1))
    return out


def chain_values(a0, b0, a1, b1, coefs):
    n = len(a0)
    f0s, e0s = [], []
    e0 = None
    for i in range(n):
        c, be, f2, e1 = coefs[i]
        if e0 is None:
            f0 = a0[i]
            e0 = b0[i]
        else:
            f0 = c * (a0[i] + a1[i] * e0)
            e0 = b0[i] + b1[i] * e0 + be * f0
        f0s.append(f0)
        e0s.append(e0)
    first, last = [None] * n, [None] * n
    first[n - 1], last[n - 1] = f0s[n - 1], e0s[n - 1]
    for i in range(n - 2, -1, -1):
        _, _, f2, e1 = coefs[i]
        first[i] = f0s[i] + f2 * first[i + 1]
        last[i] = e0s[i] + e1 * first[i + 1]
    return first, last


def kernel(
    n, nw, x_hbm, zones_hbm, coef_hbm, out_ref,
    coef_ref, x_ref, zones_ref, T, K, S, U, SX, WL, WR, Y, PP, Q, AL, GA, WW, WP, WQ, DX, D, M, V,
    rows_out, rows_lo, rows_hi, cols_out, cols_lo, cols_hi,
    cs, cr, xs, xr, wc, wv,
    in_sem, halo_send, halo_recv, a_send, a_recv, b_send, b_recv, c_send, c_recv, d_send, d_recv,
):
    depth, rows, lanes = x_ref.shape
    pz = depth // n
    bz = SX.shape[2]
    nb = depth // bz
    per = bz // pz
    me = lax.axis_index("cast")
    mw = lax.axis_index("width")
    f32 = jnp.float32

    x_copy = pltpu.make_async_copy(x_hbm, x_ref, in_sem.at[0])
    zones_copy = pltpu.make_async_copy(zones_hbm, zones_ref, in_sem.at[1])
    coef_copy = pltpu.make_async_copy(coef_hbm, coef_ref, in_sem.at[2])
    x_copy.start()
    zones_copy.start()
    coef_copy.start()

    barrier = pltpu.get_barrier_semaphore()
    for k in range(1, n):
        pl.semaphore_signal(barrier, inc=1, device_id={"cast": lax.rem(me + k, n)})
    for k in range(1, nw):
        pl.semaphore_signal(barrier, inc=1, device_id={"width": lax.rem(mw + k, nw)})

    lane2 = lax.broadcasted_iota(jnp.int32, (bz, lanes), 1)
    lane3 = lax.broadcasted_iota(jnp.int32, (rows, bz, lanes), 2)
    zero = jnp.zeros((bz, lanes), f32)
    cast_lo = (me > 0).astype(f32)
    cast_hi = (me < n - 1).astype(f32)
    width_lo = (mw > 0).astype(f32)
    width_hi = (mw < nw - 1).astype(f32)

    def pack(v, b):
        acc = zero
        for j in range(rows):
            acc = jnp.where(lane2 // 2 == j, pltpu.roll(v[j], 2 * j + 1, 1), acc)
        return pltpu.roll(acc, b * (2 * rows), 1)

    def spread(p, b, odd):
        q = pltpu.roll(p, lax.rem(lanes - b * (2 * rows), lanes), 1)
        return [
            jnp.broadcast_to(q[:, 2 * j + odd : 2 * j + odd + 1], (bz, lanes))
            for j in range(rows)
        ]

    def by_rows(ref, start):
        return [ref[pl.ds(start, bz), j, :] for j in range(rows)]

    x_copy.wait()
    rows_out[0] = x_ref[:, 0, :]
    rows_out[1] = x_ref[:, rows - 1, :]
    cols_out[...] = lax.fori_loop(
        0, nb, lambda b, acc: acc + pack(by_rows(x_ref, b * bz), b), zero
    )

    @pl.when(me == 0)
    def _():
        rows_lo[...] = jnp.zeros_like(rows_lo)

    @pl.when(me == n - 1)
    def _():
        rows_hi[...] = jnp.zeros_like(rows_hi)

    @pl.when(mw == 0)
    def _():
        cols_lo[...] = jnp.zeros_like(cols_lo)

    @pl.when(mw == nw - 1)
    def _():
        cols_hi[...] = jnp.zeros_like(cols_hi)

    def remote(src, dst, send, recv, device):
        return pltpu.make_async_remote_copy(
            src_ref=src, dst_ref=dst, send_sem=send, recv_sem=recv,
            device_id=device, device_id_type=pl.DeviceIdType.MESH,
        )

    halos = [
        (remote(rows_out.at[1], rows_lo, halo_send.at[0], halo_recv.at[0],
                {"cast": lax.rem(me + 1, n)}), me < n - 1, me > 0),
        (remote(rows_out.at[0], rows_hi, halo_send.at[1], halo_recv.at[1],
                {"cast": lax.rem(me + n - 1, n)}), me > 0, me < n - 1),
        (remote(cols_out, cols_lo, halo_send.at[2], halo_recv.at[2],
                {"width": lax.rem(mw + 1, nw)}), mw < nw - 1, mw > 0),
        (remote(cols_out, cols_hi, halo_send.at[3], halo_recv.at[3],
                {"width": lax.rem(mw + nw - 1, nw)}), mw > 0, mw < nw - 1),
    ]
    pl.semaphore_wait(barrier, n - 1 + nw - 1)
    for copy, sends, _ in halos:
        pl.when(sends)(copy.start)

    def properties(b, _):
        z = pl.ds(b * bz, bz)
        t, hot, cond = medium(x_ref[z])
        T[pl.ds(b * bz + 1, bz)] = hot
        K[pl.ds(b * bz + 1, bz)] = cond
        S[z] = 1.0 / ((1.0 - RELEASE) + RELEASE * t * t)
        U[z] = jnp.zeros((bz, rows, lanes), f32)
        for j, v in enumerate(by_rows(S, b * bz)):
            SX[b, j] = v
        return 0

    lax.fori_loop(0, nb, properties, 0)
    T[0], T[depth + 1] = T[1], T[depth]
    K[0], K[depth + 1] = -K[1], -K[depth]
    zones_copy.wait()
    coef_copy.wait()
    for side, plane in ((0, 0), (1, depth - 1)):
        zone = zones_ref[side]
        coef = jnp.zeros((rows, lanes), f32)
        for i in range(coef_ref.shape[0]):
            coef = jnp.where(zone == i, coef_ref[i], coef)
        U[plane] = coef * (depth * depth / 8.0)

    for copy, _, receives in halos:
        pl.when(receives)(copy.wait_recv)

    gain_cast = rows * rows * 4.0 * 0.5
    gain_width = lanes * lanes / 4.0 * 0.5
    gain_thick = depth * depth / 4.0 * 0.5
    width_lo_mask = jnp.where(lane2 == 0, width_lo, 1.0)
    width_hi_mask = jnp.where(lane2 == lanes - 1, width_hi, 1.0)
    _, col_lo_T, col_lo_K = medium(cols_lo[...])
    _, col_hi_T, col_hi_K = medium(cols_hi[...])

    def gather_copy(dest):
        return remote(cs.at[dest], cr.at[me], a_send.at[dest], a_recv.at[me], {"cast": dest})

    def gather_wait(source):
        remote(cs.at[source], cr.at[source], a_send.at[source], a_recv.at[source],
               {"cast": source}).wait_recv()

    def cast_block(k, _):
        b = lax.rem(me // per + nb // 2 + k, nb)
        start = pl.multiple_of(b * bz, bz)
        hot, cond = by_rows(T, start + 1), by_rows(K, start + 1)
        hot_m, cond_m = by_rows(T, start), by_rows(K, start)
        hot_p, cond_p = by_rows(T, start + 2), by_rows(K, start + 2)
        surf = by_rows(U, start)
        _, hot_lo, cond_lo = medium(rows_lo[pl.ds(start, bz), :])
        _, hot_hi, cond_hi = medium(rows_hi[pl.ds(start, bz), :])
        hots, conds = [hot_lo] + hot + [hot_hi], [cond_lo] + cond + [cond_hi]
        faces = [gain_cast * (conds[j] + conds[j + 1]) for j in range(rows + 1)]
        faces[0], faces[rows] = faces[0] * cast_lo, faces[rows] * cast_hi
        flux = [faces[j] * (hots[j + 1] - hots[j]) for j in range(rows + 1)]

        lo_T, lo_K = spread(col_lo_T, b, 0), spread(col_lo_K, b, 0)
        hi_T, hi_K = spread(col_hi_T, b, 1), spread(col_hi_K, b, 1)
        r = []
        for j in range(rows):
            h, c = hot[j], cond[j]
            hm = jnp.where(lane2 == 0, lo_T[j], pltpu.roll(h, 1, 1))
            cm = jnp.where(lane2 == 0, lo_K[j], pltpu.roll(c, 1, 1))
            hp = jnp.where(lane2 == lanes - 1, hi_T[j], pltpu.roll(h, lanes - 1, 1))
            cp = jnp.where(lane2 == lanes - 1, hi_K[j], pltpu.roll(c, lanes - 1, 1))
            lo = gain_width * (c + cm) * width_lo_mask
            hi = gain_width * (c + cp) * width_hi_mask
            WL[b, j] = lo
            WR[b, j] = hi
            r.append(
                surf[j] * (MEDIUM - h)
                + (flux[j + 1] - flux[j])
                + (hi * (hp - h) - lo * (h - hm))
                + gain_thick
                * ((c + cond_p[j]) * (hot_p[j] - h) - (c + cond_m[j]) * (h - hot_m[j]))
            )
        s = [SX[b, j] for j in range(rows)]
        ys, ps, qs = row_levels(s, faces[1:rows], faces[0], faces[rows], r)
        for j in range(rows):
            Y[b, j] = ys[j]
            PP[b, j] = ps[j]
            Q[b, j] = qs[j]
        for o in range(per):
            dest = b * per + o
            for v, value in enumerate((ys[0], ps[0], qs[0], ys[-1], ps[-1], qs[-1])):
                cs[dest, v * pz : (v + 1) * pz] = value[o * pz : (o + 1) * pz]

            @pl.when(dest != me)
            def _():
                gather_copy(dest).start()

        return 0

    lax.fori_loop(0, nb, cast_block, 0)
    cr[me] = cs[me]

    def width_block(b, carry):
        lo, hi = WL[b], WR[b]
        left = jnp.where(lane3 == 0, lo, 0.0)
        right = jnp.where(lane3 == lanes - 1, hi, 0.0)
        ground, left, right, factors = lane_levels(
            SX[b] + left + right, lo - left, hi - right, left, right
        )
        for i, (al, ga) in enumerate(factors):
            AL[i, b] = al
            GA[i, b] = ga
        w = 1.0 / ground
        p, q = left * w, right * w
        WW[b], WP[b], WQ[b] = w, p, q
        return carry[0] + pack(p, b), carry[1] + pack(q, b)

    p_ends, q_ends = lax.fori_loop(0, nb, width_block, (zero, zero))
    wc[mw, 0] = p_ends
    wc[mw, 1] = q_ends
    wide_coefs = [
        remote(wc.at[mw], wc.at[mw], c_send.at[k - 1], c_recv.at[k - 1],
               {"width": lax.rem(mw + k, nw)})
        for k in range(1, nw)
    ]
    for copy in wide_coefs:
        copy.start()

    for i in range(n):
        pl.when(me != i)(functools.partial(gather_wait, i))
    got = [[cr[i, v * pz : (v + 1) * pz] for v in range(6)] for i in range(n)]
    a0, a1, a2, b0, b1, b2 = [[got[i][v] for i in range(n)] for v in range(6)]
    first, last = chain_values(a0, b0, a1, b1, chain_coefs(a1, a2, b1, b2))
    blank = jnp.zeros_like(first[0])

    def answer_copy(i):
        return remote(xs.at[i], xr.at[me], b_send.at[i], b_recv.at[me], {"cast": i})

    for i in range(n):
        xs[i, 0:pz] = last[i - 1] if i > 0 else blank
        xs[i, pz : 2 * pz] = first[i + 1] if i < n - 1 else blank
        pl.when(me != i)(answer_copy(i).start)
    xr[me] = xs[me]

    half = depth // 2
    zlo_sum, zhi_sum = S[0] + U[0], S[depth - 1] + U[depth - 1]
    for i in range(half - 1):
        j = depth - 1 - i
        glo, ghi = gain_thick * (K[i + 1] + K[i + 2]), gain_thick * (K[j] + K[j + 1])
        wlo, whi = 1.0 / (zlo_sum + glo), 1.0 / (zhi_sum + ghi)
        mlo, mhi = glo * wlo, ghi * whi
        M[i], M[j] = mlo, mhi
        V[i], V[j] = wlo, whi
        zlo_sum = S[i + 1] + mlo * zlo_sum
        zhi_sum = S[j - 1] + mhi * zhi_sum
    gmid = gain_thick * (K[half] + K[half + 1])
    det = 1.0 / (zlo_sum * zhi_sum + gmid * (zlo_sum + zhi_sum))
    V[half - 1] = (zhi_sum + gmid) * det
    V[half] = (zlo_sum + gmid) * det
    M[half] = gmid * det

    def step_block(k, carry):
        b = lax.rem(me // per + k, nb)
        los, his = [], []
        for o in range(per):
            owner = b * per + o

            @pl.when(owner != me)
            def _():
                remote(xs.at[owner], xr.at[owner], b_send.at[owner], b_recv.at[owner],
                       {"cast": owner}).wait_recv()

            los.append(xr[owner, 0:pz])
            his.append(xr[owner, pz : 2 * pz])
        lo = los[0] if per == 1 else jnp.concatenate(los, 0)
        hi = his[0] if per == 1 else jnp.concatenate(his, 0)
        r = (Y[b] + PP[b] * lo[None] + Q[b] * hi[None]) * SX[b]
        step, i = 1, 0
        while step < lanes:
            r = apply_level(r, AL[i, b], GA[i, b], step, 2)
            step, i = step * 2, i + 1
        r = r * WW[b]
        DX[b] = r
        return carry + pack(r, b)

    wv[mw] = lax.fori_loop(0, nb, step_block, zero)
    wide_values = [
        remote(wv.at[mw], wv.at[mw], d_send.at[k - 1], d_recv.at[k - 1],
               {"width": lax.rem(mw + k, nw)})
        for k in range(1, nw)
    ]
    for copy in wide_values:
        copy.start()

    for copy in wide_coefs:
        copy.wait_recv()

    def firsts(p):
        return pltpu.roll(p, lanes - 1, 1)

    even = lane2 % 2 == 0
    b1 = [jnp.where(even, wc[i, 0], 0.0) for i in range(nw)]
    b2 = [jnp.where(even, wc[i, 1], 0.0) for i in range(nw)]
    a1 = [jnp.where(even, firsts(wc[i, 0]), 0.0) for i in range(nw)]
    a2 = [jnp.where(even, firsts(wc[i, 1]), 0.0) for i in range(nw)]
    coefs = chain_coefs(a1, a2, b1, b2)
    for copy in wide_values:
        copy.wait_recv()
    b0 = [wv[i] for i in range(nw)]
    a0 = [firsts(b0[i]) for i in range(nw)]
    first, last = chain_values(a0, b0, a1, b1, coefs)
    before, after = zero, zero
    for i in range(nw):
        if i > 0:
            before = jnp.where(mw == i, last[i - 1], before)
        if i < nw - 1:
            after = jnp.where(mw == i, first[i + 1], after)

    def thick_block(b, _):
        start = b * bz
        los, his = spread(before, b, 0), spread(after, b, 0)
        for j in range(rows):
            D[pl.ds(start, bz), j, :] = (DX[b, j] + WP[b, j] * los[j] + WQ[b, j] * his[j]) * SX[
                b, j
            ]
        return 0

    lax.fori_loop(0, nb, thick_block, 0)

    dlo, dhi = D[0], D[depth - 1]
    for i in range(half - 1):
        j = depth - 1 - i
        D[i], D[j] = dlo, dhi
        dlo = D[i + 1] + M[i] * dlo
        dhi = D[j - 1] + M[j] * dhi
    ulo = V[half - 1] * dlo + M[half] * dhi
    uhi = V[half] * dhi + M[half] * dlo
    out_ref[half - 1] = ulo * S[half - 1]
    out_ref[half] = uhi * S[half]
    for i in range(half - 2, -1, -1):
        j = depth - 1 - i
        ulo = V[i] * D[i] + M[i] * ulo
        uhi = V[j] * D[j] + M[j] * uhi
        out_ref[i] = ulo * S[i]
        out_ref[j] = uhi * S[j]

    for copy, sends, _ in halos:
        pl.when(sends)(copy.wait_send)
    for i in range(n):
        pl.when(me != i)(gather_copy(i).wait_send)
    for i in range(n):
        pl.when(me != i)(answer_copy(i).wait_send)
    for copy in wide_coefs + wide_values:
        copy.wait_send()


def shards(n, nw, x, zones, spray_coef):
    depth, rows, lanes = x.shape
    pz = depth // n
    f32 = jnp.float32
    vmem = pltpu.VMEM
    bz = max(pz, depth // 2)
    nb = depth // bz
    field = vmem((depth, rows, lanes), f32)
    blocks = vmem((nb, rows, bz, lanes), f32)
    padded = vmem((depth + 2, rows, lanes), f32)
    levels = vmem(((lanes - 1).bit_length(), nb, rows, bz, lanes), f32)
    edge = vmem((depth, lanes), f32)
    packed = vmem((bz, lanes), f32)
    dma = pltpu.SemaphoreType.DMA
    scratch = (
        [pltpu.SMEM(spray_coef.shape, f32)]
        + [field, vmem(zones.shape, zones.dtype), padded, padded]
        + [field, field]
        + [blocks] * 6
        + [levels, levels]
        + [blocks] * 4
        + [field] * 3
        + [vmem((2, depth, lanes), f32), edge, edge, packed, packed, packed]
        + [
            vmem((n, 6 * pz, lanes), f32),
            vmem((n, 6 * pz, lanes), f32),
            vmem((n, 2 * pz, lanes), f32),
            vmem((n, 2 * pz, lanes), f32),
            vmem((nw, 2, bz, lanes), f32),
            vmem((nw, bz, lanes), f32),
        ]
        + [dma((3,)), dma((4,)), dma((4,))]
        + [dma((n,))] * 4
        + [dma((nw,))] * 4
    )
    step = pl.pallas_call(
        functools.partial(kernel, n, nw),
        out_shape=jax.ShapeDtypeStruct(x.shape, f32),
        in_specs=[
            pl.BlockSpec(memory_space=pltpu.HBM),
            pl.BlockSpec(memory_space=pltpu.HBM),
            pl.BlockSpec(memory_space=pltpu.HBM),
        ],
        out_specs=pl.BlockSpec(memory_space=pltpu.VMEM),
        scratch_shapes=scratch,
        compiler_params=pltpu.CompilerParams(
            collective_id=0, has_side_effects=True, vmem_limit_bytes=63 * 1024 * 1024
        ),
        cost_estimate=pl.CostEstimate(
            flops=20_000_000, bytes_accessed=1_000_000, transcendentals=100_000
        ),
        name="adi_step",
    )(x, zones, spray_coef)
    return x + step


def solution(mesh):
    spec = P(None, "cast", "width")
    body = functools.partial(shards, mesh.shape["cast"], mesh.shape["width"])
    return jax.shard_map(
        body, mesh=mesh, in_specs=(spec, spec, P()), out_specs=spec, check_vma=False
    )
```

```python
import functools

import jax
import jax.numpy as jnp
from jax import lax
from jax.experimental import pallas as pl
from jax.experimental.pallas import tpu as pltpu
from jax.sharding import PartitionSpec as P

RELEASE = 0.4
MEDIUM = -2.0


def medium(x):
    t = jnp.tanh(x)
    hot = x - RELEASE * t
    cond = 1.5 - 0.5 * jnp.tanh(hot)
    return t, hot, cond


def lane_levels(ground, gl, gr, left, right):
    axis = ground.ndim - 1
    size = ground.shape[axis]
    lane = lax.broadcasted_iota(jnp.int32, ground.shape, axis)
    ends = left + right
    factors = []
    step = 1
    while step < size:
        w = 1.0 / (ground + gl + gr)
        al = gl * pltpu.roll(w, step, axis)
        ga = gr * pltpu.roll(w, size - step, axis)
        factors.append((al, ga))
        ground = (
            ground
            + al * pltpu.roll(ground, step, axis)
            + ga * pltpu.roll(ground, size - step, axis)
        )
        from_left = al * pltpu.roll(ends, step, axis)
        from_right = ga * pltpu.roll(ends, size - step, axis)
        if 2 * step < size:
            ends = ends + from_left + from_right
            gl = al * pltpu.roll(gl, step, axis)
            gr = ga * pltpu.roll(gr, size - step, axis)
        else:
            left = jnp.where(lane < step, ends, 0.0) + from_left
            right = jnp.where(lane >= step, ends, 0.0) + from_right
        step *= 2
    return ground, left, right, factors


def row_levels(ground, links, left, right, r):
    count = len(ground)
    zero = jnp.zeros_like(left)
    ground = list(ground)
    ground[0] = ground[0] + left
    ground[-1] = ground[-1] + right
    lefts = [left] + [zero] * (count - 1)
    rights = [zero] * (count - 1) + [right]
    step = 1
    while step < count:
        w = []
        for j in range(count):
            total = ground[j]
            if j >= step:
                total = total + links[j - step]
            if j + step < count:
                total = total + links[j]
            w.append(1.0 / total)
        new_ground, new_r = list(ground), list(r)
        new_left, new_right = list(lefts), list(rights)
        new_links = [None] * count
        for j in range(count):
            if j >= step:
                al = links[j - step] * w[j - step]
                new_ground[j] = new_ground[j] + al * ground[j - step]
                new_r[j] = new_r[j] + al * r[j - step]
                if j - step < step:
                    new_left[j] = new_left[j] + al * lefts[j - step]
                if j >= 2 * step:
                    new_links[j - 2 * step] = al * links[j - 2 * step]
            if j + step < count:
                ga = links[j] * w[j + step]
                new_ground[j] = new_ground[j] + ga * ground[j + step]
                new_r[j] = new_r[j] + ga * r[j + step]
                if j + step >= count - step:
                    new_right[j] = new_right[j] + ga * rights[j + step]
        ground, r, lefts, rights, links = new_ground, new_r, new_left, new_right, new_links
        step *= 2
    w = [1.0 / g for g in ground]
    return [[a * b for a, b in zip(v, w)] for v in (r, lefts, rights)]


def apply_level(r, al, ga, step, axis):
    size = r.shape[axis]
    return r + al * pltpu.roll(r, step, axis) + ga * pltpu.roll(r, size - step, axis)


def half_coefs(a1, a2, b1, b2):
    out = [(None, None, a2[0], b2[0])]
    for i in range(1, len(a1)):
        e1 = out[-1][3]
        c = 1.0 / (1.0 - a1[i] * e1)
        be = b1[i] * e1
        f2 = c * a2[i]
        out.append((c, be, f2, be * f2 + b2[i]))
    return out


def half_values(a0, b0, a1, b1, coefs):
    out = [(a0[0], b0[0])]
    for i in range(1, len(a0)):
        c, be, _, _ = coefs[i]
        e0 = out[-1][1]
        f0 = c * (a0[i] + a1[i] * e0)
        out.append((f0, b0[i] + b1[i] * e0 + be * f0))
    return out


def half_back(values, coefs, beyond):
    first, last = [], []
    for (f0, e0), (_, _, f2, e1) in zip(reversed(values), reversed(coefs)):
        last.append(e0 + e1 * beyond)
        beyond = f0 + f2 * beyond
        first.append(beyond)
    return first[::-1], last[::-1]


def chain_coefs(a1, a2, b1, b2):
    m = len(a1) // 2
    low = half_coefs(a1[:m], a2[:m], b1[:m], b2[:m])
    high = half_coefs(b2[m:][::-1], b1[m:][::-1], a2[m:][::-1], a1[m:][::-1])
    return low, high, 1.0 / (1.0 - low[-1][3] * high[-1][3])


def chain_values(a0, b0, a1, a2, b1, b2, coefs):
    m = len(a0) // 2
    low, high, c = coefs
    low_values = half_values(a0[:m], b0[:m], a1[:m], b1[:m], low)
    high_values = half_values(b0[m:][::-1], a0[m:][::-1], b2[m:][::-1], a2[m:][::-1], high)
    low_end, high_end = low_values[-1][1], high_values[-1][1]
    end = c * (low_end + low[-1][3] * high_end)
    start = high_end + high[-1][3] * end
    first, last = half_back(low_values, low, start)
    last_high, first_high = half_back(high_values, high, end)
    return first + first_high[::-1], last + last_high[::-1]


def kernel(
    n, nw, x_hbm, zones_hbm, coef_hbm, out_ref,
    coef_ref, x_ref, zones_ref, T, K, S, U, SX, WL, WR, Y, PP, Q, AL, GA, WW, WP, WQ, DX, D, M, V,
    rows_out, rows_lo, rows_hi, cols_out, cols_lo, cols_hi,
    cs, cr, xs, xr, wc, wv,
    in_sem, halo_send, halo_recv, a_send, a_recv, b_send, b_recv, c_send, c_recv, d_send, d_recv,
):
    depth, rows, lanes = x_ref.shape
    pz = depth // n
    bz = SX.shape[2]
    nb = depth // bz
    per = bz // pz
    me = lax.axis_index("cast")
    mw = lax.axis_index("width")
    f32 = jnp.float32

    x_copy = pltpu.make_async_copy(x_hbm, x_ref, in_sem.at[0])
    zones_copy = pltpu.make_async_copy(zones_hbm, zones_ref, in_sem.at[1])
    coef_copy = pltpu.make_async_copy(coef_hbm, coef_ref, in_sem.at[2])
    x_copy.start()
    zones_copy.start()
    coef_copy.start()

    barrier = pltpu.get_barrier_semaphore()
    for k in range(1, n):
        pl.semaphore_signal(barrier, inc=1, device_id={"cast": lax.rem(me + k, n)})
    for k in range(1, nw):
        pl.semaphore_signal(barrier, inc=1, device_id={"width": lax.rem(mw + k, nw)})

    lane2 = lax.broadcasted_iota(jnp.int32, (bz, lanes), 1)
    zero = jnp.zeros((bz, lanes), f32)
    cast_lo = (me > 0).astype(f32)
    cast_hi = (me < n - 1).astype(f32)
    width_lo = (mw > 0).astype(f32)
    width_hi = (mw < nw - 1).astype(f32)

    def pack(v, b):
        acc = zero
        for j in range(rows):
            acc = jnp.where(lane2 // 2 == j, pltpu.roll(v[j], 2 * j + 1, 1), acc)
        return acc if isinstance(b, int) and b == 0 else pltpu.roll(acc, b * (2 * rows), 1)

    def spread(p, b, odd):
        q = pltpu.roll(p, lax.rem(lanes - b * (2 * rows), lanes), 1)
        return [
            jnp.broadcast_to(q[:, 2 * j + odd : 2 * j + odd + 1], (bz, lanes))
            for j in range(rows)
        ]

    def by_rows(ref, start):
        return [ref[pl.ds(start, bz), j, :] for j in range(rows)]

    x_copy.wait()
    rows_out[0] = x_ref[:, 0, :]
    rows_out[1] = x_ref[:, rows - 1, :]
    cols_out[...] = lax.fori_loop(
        0, nb, lambda b, acc: acc + pack(by_rows(x_ref, b * bz), b), zero
    )

    @pl.when(me == 0)
    def _():
        rows_lo[...] = jnp.zeros_like(rows_lo)

    @pl.when(me == n - 1)
    def _():
        rows_hi[...] = jnp.zeros_like(rows_hi)

    @pl.when(mw == 0)
    def _():
        cols_lo[...] = jnp.zeros_like(cols_lo)

    @pl.when(mw == nw - 1)
    def _():
        cols_hi[...] = jnp.zeros_like(cols_hi)

    def remote(src, dst, send, recv, device):
        return pltpu.make_async_remote_copy(
            src_ref=src, dst_ref=dst, send_sem=send, recv_sem=recv,
            device_id=device, device_id_type=pl.DeviceIdType.MESH,
        )

    halos = [
        (remote(rows_out.at[1], rows_lo, halo_send.at[0], halo_recv.at[0],
                {"cast": lax.rem(me + 1, n)}), me < n - 1, me > 0),
        (remote(rows_out.at[0], rows_hi, halo_send.at[1], halo_recv.at[1],
                {"cast": lax.rem(me + n - 1, n)}), me > 0, me < n - 1),
        (remote(cols_out, cols_lo, halo_send.at[2], halo_recv.at[2],
                {"width": lax.rem(mw + 1, nw)}), mw < nw - 1, mw > 0),
        (remote(cols_out, cols_hi, halo_send.at[3], halo_recv.at[3],
                {"width": lax.rem(mw + nw - 1, nw)}), mw > 0, mw < nw - 1),
    ]
    pl.semaphore_wait(barrier, n - 1 + nw - 1)
    for copy, sends, _ in halos:
        pl.when(sends)(copy.start)

    def properties(b, _):
        z = pl.ds(b * bz, bz)
        t, hot, cond = medium(x_ref[z])
        T[pl.ds(b * bz + 1, bz)] = hot
        K[pl.ds(b * bz + 1, bz)] = cond
        S[z] = 1.0 / ((1.0 - RELEASE) + RELEASE * t * t)
        U[z] = jnp.zeros((bz, rows, lanes), f32)
        for j, v in enumerate(by_rows(S, b * bz)):
            SX[b, j] = v
        return 0

    lax.fori_loop(0, nb, properties, 0)
    T[0], T[depth + 1] = T[1], T[depth]
    K[0], K[depth + 1] = -K[1], -K[depth]
    zones_copy.wait()
    coef_copy.wait()
    for side, plane in ((0, 0), (1, depth - 1)):
        zone = zones_ref[side]
        coef = jnp.zeros((rows, lanes), f32)
        for i in range(coef_ref.shape[0]):
            coef = jnp.where(zone == i, coef_ref[i], coef)
        U[plane] = coef * (depth * depth / 8.0)

    for copy, _, receives in halos:
        pl.when(receives)(copy.wait_recv)

    gain_cast = rows * rows * 4.0 * 0.5
    gain_width = lanes * lanes / 4.0 * 0.5
    gain_thick = depth * depth / 4.0 * 0.5
    width_lo_mask = jnp.where(lane2 == 0, width_lo, 1.0)
    width_hi_mask = jnp.where(lane2 == lanes - 1, width_hi, 1.0)
    _, col_lo_T, col_lo_K = medium(cols_lo[...])
    _, col_hi_T, col_hi_K = medium(cols_hi[...])

    def gather_copy(dest):
        return remote(cs.at[dest], cr.at[me], a_send.at[dest], a_recv.at[me], {"cast": dest})

    def gather_wait(source):
        remote(cs.at[source], cr.at[source], a_send.at[source], a_recv.at[source],
               {"cast": source}).wait_recv()

    def cast_block(k, _):
        b = lax.rem(me // per + nb // 2 + k, nb)
        start = pl.multiple_of(b * bz, bz)
        hot, cond = by_rows(T, start + 1), by_rows(K, start + 1)
        hot_m, cond_m = by_rows(T, start), by_rows(K, start)
        hot_p, cond_p = by_rows(T, start + 2), by_rows(K, start + 2)
        surf = by_rows(U, start)
        _, hot_lo, cond_lo = medium(rows_lo[pl.ds(start, bz), :])
        _, hot_hi, cond_hi = medium(rows_hi[pl.ds(start, bz), :])
        hots, conds = [hot_lo] + hot + [hot_hi], [cond_lo] + cond + [cond_hi]
        faces = [gain_cast * (conds[j] + conds[j + 1]) for j in range(rows + 1)]
        faces[0], faces[rows] = faces[0] * cast_lo, faces[rows] * cast_hi
        flux = [faces[j] * (hots[j + 1] - hots[j]) for j in range(rows + 1)]

        lo_T, lo_K = spread(col_lo_T, b, 0), spread(col_lo_K, b, 0)
        hi_T, hi_K = spread(col_hi_T, b, 1), spread(col_hi_K, b, 1)
        r = []
        for j in range(rows):
            h, c = hot[j], cond[j]
            hm = jnp.where(lane2 == 0, lo_T[j], pltpu.roll(h, 1, 1))
            cm = jnp.where(lane2 == 0, lo_K[j], pltpu.roll(c, 1, 1))
            hp = jnp.where(lane2 == lanes - 1, hi_T[j], pltpu.roll(h, lanes - 1, 1))
            cp = jnp.where(lane2 == lanes - 1, hi_K[j], pltpu.roll(c, lanes - 1, 1))
            lo = gain_width * (c + cm) * width_lo_mask
            hi = gain_width * (c + cp) * width_hi_mask
            WL[b, j] = lo
            WR[b, j] = hi
            r.append(
                surf[j] * (MEDIUM - h)
                + (flux[j + 1] - flux[j])
                + (hi * (hp - h) - lo * (h - hm))
                + gain_thick
                * ((c + cond_p[j]) * (hot_p[j] - h) - (c + cond_m[j]) * (h - hot_m[j]))
            )
        s = [SX[b, j] for j in range(rows)]
        ys, ps, qs = row_levels(s, faces[1:rows], faces[0], faces[rows], r)
        for j in range(rows):
            Y[b, j] = ys[j]
            PP[b, j] = ps[j]
            Q[b, j] = qs[j]
        for o in range(per):
            dest = b * per + o
            for v, value in enumerate((ys[0], ps[0], qs[0], ys[-1], ps[-1], qs[-1])):
                cs[dest, v * pz : (v + 1) * pz] = value[o * pz : (o + 1) * pz]

            @pl.when(dest != me)
            def _():
                gather_copy(dest).start()

        return 0

    lax.fori_loop(0, nb, cast_block, 0)
    cr[me] = cs[me]

    lane4 = lax.broadcasted_iota(jnp.int32, SX.shape, 3)
    lo, hi = WL[...], WR[...]
    left = jnp.where(lane4 == 0, lo, 0.0)
    right = jnp.where(lane4 == lanes - 1, hi, 0.0)
    ground, left, right, factors = lane_levels(
        SX[...] + left + right, lo - left, hi - right, left, right
    )
    for i, (al, ga) in enumerate(factors):
        AL[i] = al
        GA[i] = ga
    w = 1.0 / ground
    p, q = left * w, right * w
    WW[...], WP[...], WQ[...] = w, p, q
    p_ends = sum(pack(p[b], b) for b in range(nb))
    q_ends = sum(pack(q[b], b) for b in range(nb))
    wc[mw, 0] = p_ends
    wc[mw, 1] = q_ends
    wide_coefs = [
        remote(wc.at[mw], wc.at[mw], c_send.at[k - 1], c_recv.at[k - 1],
               {"width": lax.rem(mw + k, nw)})
        for k in range(1, nw)
    ]
    for copy in wide_coefs:
        copy.start()

    for i in range(n):
        pl.when(me != i)(functools.partial(gather_wait, i))
    got = [[cr[i, v * pz : (v + 1) * pz] for v in range(6)] for i in range(n)]
    a0, a1, a2, b0, b1, b2 = [[got[i][v] for i in range(n)] for v in range(6)]
    first, last = chain_values(
        a0, b0, a1, a2, b1, b2, chain_coefs(a1, a2, b1, b2)
    )
    blank = jnp.zeros_like(first[0])

    def answer_copy(i):
        return remote(xs.at[i], xr.at[me], b_send.at[i], b_recv.at[me], {"cast": i})

    for i in range(n):
        xs[i, 0:pz] = last[i - 1] if i > 0 else blank
        xs[i, pz : 2 * pz] = first[i + 1] if i < n - 1 else blank
        pl.when(me != i)(answer_copy(i).start)
    xr[me] = xs[me]

    half = depth // 2
    zlo_sum, zhi_sum = S[0] + U[0], S[depth - 1] + U[depth - 1]
    for i in range(half - 1):
        j = depth - 1 - i
        glo, ghi = gain_thick * (K[i + 1] + K[i + 2]), gain_thick * (K[j] + K[j + 1])
        wlo, whi = 1.0 / (zlo_sum + glo), 1.0 / (zhi_sum + ghi)
        mlo, mhi = glo * wlo, ghi * whi
        M[i], M[j] = mlo, mhi
        V[i], V[j] = wlo, whi
        zlo_sum = S[i + 1] + mlo * zlo_sum
        zhi_sum = S[j - 1] + mhi * zhi_sum
    gmid = gain_thick * (K[half] + K[half + 1])
    det = 1.0 / (zlo_sum * zhi_sum + gmid * (zlo_sum + zhi_sum))
    V[half - 1] = (zhi_sum + gmid) * det
    V[half] = (zlo_sum + gmid) * det
    M[half] = gmid * det

    def answer_wait(i):
        remote(xs.at[i], xr.at[i], b_send.at[i], b_recv.at[i], {"cast": i}).wait_recv()

    for i in range(n):
        pl.when(me != i)(functools.partial(answer_wait, i))
    los = jnp.concatenate([xr[i, 0:pz] for i in range(n)], 0).reshape(nb, 1, bz, lanes)
    his = jnp.concatenate([xr[i, pz : 2 * pz] for i in range(n)], 0).reshape(nb, 1, bz, lanes)
    r = (Y[...] + PP[...] * los + Q[...] * his) * SX[...]
    step, i = 1, 0
    while step < lanes:
        r = apply_level(r, AL[i], GA[i], step, 3)
        step, i = step * 2, i + 1
    r = r * WW[...]
    DX[...] = r
    wv[mw] = sum(pack(r[b], b) for b in range(nb))
    wide_values = [
        remote(wv.at[mw], wv.at[mw], d_send.at[k - 1], d_recv.at[k - 1],
               {"width": lax.rem(mw + k, nw)})
        for k in range(1, nw)
    ]
    for copy in wide_values:
        copy.start()

    for copy in wide_coefs:
        copy.wait_recv()

    def firsts(p):
        return pltpu.roll(p, lanes - 1, 1)

    even = lane2 % 2 == 0
    b1 = [jnp.where(even, wc[i, 0], 0.0) for i in range(nw)]
    b2 = [jnp.where(even, wc[i, 1], 0.0) for i in range(nw)]
    a1 = [jnp.where(even, firsts(wc[i, 0]), 0.0) for i in range(nw)]
    a2 = [jnp.where(even, firsts(wc[i, 1]), 0.0) for i in range(nw)]
    coefs = chain_coefs(a1, a2, b1, b2)
    for copy in wide_values:
        copy.wait_recv()
    b0 = [wv[i] for i in range(nw)]
    a0 = [firsts(b0[i]) for i in range(nw)]
    first, last = chain_values(a0, b0, a1, a2, b1, b2, coefs)
    before, after = zero, zero
    for i in range(nw):
        if i > 0:
            before = jnp.where(mw == i, last[i - 1], before)
        if i < nw - 1:
            after = jnp.where(mw == i, first[i + 1], after)

    def thick_block(b, _):
        start = b * bz
        los, his = spread(before, b, 0), spread(after, b, 0)
        for j in range(rows):
            D[pl.ds(start, bz), j, :] = (DX[b, j] + WP[b, j] * los[j] + WQ[b, j] * his[j]) * SX[
                b, j
            ]
        return 0

    lax.fori_loop(0, nb, thick_block, 0)

    dlo, dhi = D[0], D[depth - 1]
    for i in range(half - 1):
        j = depth - 1 - i
        D[i], D[j] = dlo, dhi
        dlo = D[i + 1] + M[i] * dlo
        dhi = D[j - 1] + M[j] * dhi
    ulo = V[half - 1] * dlo + M[half] * dhi
    uhi = V[half] * dhi + M[half] * dlo
    out_ref[half - 1] = ulo * S[half - 1]
    out_ref[half] = uhi * S[half]
    for i in range(half - 2, -1, -1):
        j = depth - 1 - i
        ulo = V[i] * D[i] + M[i] * ulo
        uhi = V[j] * D[j] + M[j] * uhi
        out_ref[i] = ulo * S[i]
        out_ref[j] = uhi * S[j]

    for copy, sends, _ in halos:
        pl.when(sends)(copy.wait_send)
    for i in range(n):
        pl.when(me != i)(gather_copy(i).wait_send)
    for i in range(n):
        pl.when(me != i)(answer_copy(i).wait_send)
    for copy in wide_coefs + wide_values:
        copy.wait_send()


def shards(n, nw, x, zones, spray_coef):
    depth, rows, lanes = x.shape
    pz = depth // n
    f32 = jnp.float32
    vmem = pltpu.VMEM
    bz = max(pz, depth // 2)
    nb = depth // bz
    field = vmem((depth, rows, lanes), f32)
    blocks = vmem((nb, rows, bz, lanes), f32)
    padded = vmem((depth + 2, rows, lanes), f32)
    levels = vmem(((lanes - 1).bit_length(), nb, rows, bz, lanes), f32)
    edge = vmem((depth, lanes), f32)
    packed = vmem((bz, lanes), f32)
    dma = pltpu.SemaphoreType.DMA
    scratch = (
        [pltpu.SMEM(spray_coef.shape, f32)]
        + [field, vmem(zones.shape, zones.dtype), padded, padded]
        + [field, field]
        + [blocks] * 6
        + [levels, levels]
        + [blocks] * 4
        + [field] * 3
        + [vmem((2, depth, lanes), f32), edge, edge, packed, packed, packed]
        + [
            vmem((n, 6 * pz, lanes), f32),
            vmem((n, 6 * pz, lanes), f32),
            vmem((n, 2 * pz, lanes), f32),
            vmem((n, 2 * pz, lanes), f32),
            vmem((nw, 2, bz, lanes), f32),
            vmem((nw, bz, lanes), f32),
        ]
        + [dma((3,)), dma((4,)), dma((4,))]
        + [dma((n,))] * 4
        + [dma((nw,))] * 4
    )
    step = pl.pallas_call(
        functools.partial(kernel, n, nw),
        out_shape=jax.ShapeDtypeStruct(x.shape, f32),
        in_specs=[
            pl.BlockSpec(memory_space=pltpu.HBM),
            pl.BlockSpec(memory_space=pltpu.HBM),
            pl.BlockSpec(memory_space=pltpu.HBM),
        ],
        out_specs=pl.BlockSpec(memory_space=pltpu.VMEM),
        scratch_shapes=scratch,
        compiler_params=pltpu.CompilerParams(
            collective_id=0, has_side_effects=True, vmem_limit_bytes=63 * 1024 * 1024
        ),
        cost_estimate=pl.CostEstimate(
            flops=20_000_000, bytes_accessed=1_000_000, transcendentals=100_000
        ),
        name="adi_step",
    )(x, zones, spray_coef)
    return x + step


def solution(mesh):
    spec = P(None, "cast", "width")
    body = functools.partial(shards, mesh.shape["cast"], mesh.shape["width"])
    return jax.shard_map(
        body, mesh=mesh, in_specs=(spec, spec, P()), out_specs=spec, check_vma=False
    )
```

```python
import functools

import jax
import jax.numpy as jnp
from jax import lax
from jax.experimental import pallas as pl
from jax.experimental.pallas import tpu as pltpu
from jax.sharding import PartitionSpec as P

RELEASE = 0.4
MEDIUM = -2.0


def medium(x):
    t = jnp.tanh(x)
    hot = x - RELEASE * t
    cond = 1.5 - 0.5 * jnp.tanh(hot)
    return t, hot, cond


def lane_levels(ground, gl, gr, left, right):
    axis = ground.ndim - 1
    size = ground.shape[axis]
    lane = lax.broadcasted_iota(jnp.int32, ground.shape, axis)
    ends = left + right
    factors = []
    step = 1
    while step < size:
        w = 1.0 / (ground + gl + gr)
        al = gl * pltpu.roll(w, step, axis)
        ga = gr * pltpu.roll(w, size - step, axis)
        factors.append((al, ga))
        ground = (
            ground
            + al * pltpu.roll(ground, step, axis)
            + ga * pltpu.roll(ground, size - step, axis)
        )
        from_left = al * pltpu.roll(ends, step, axis)
        from_right = ga * pltpu.roll(ends, size - step, axis)
        if 2 * step < size:
            ends = ends + from_left + from_right
            gl = al * pltpu.roll(gl, step, axis)
            gr = ga * pltpu.roll(gr, size - step, axis)
        else:
            left = jnp.where(lane < step, ends, 0.0) + from_left
            right = jnp.where(lane >= step, ends, 0.0) + from_right
        step *= 2
    return ground, left, right, factors


def row_levels(ground, links, left, right, r):
    count = len(ground)
    zero = jnp.zeros_like(left)
    ground = list(ground)
    ground[0] = ground[0] + left
    ground[-1] = ground[-1] + right
    lefts = [left] + [zero] * (count - 1)
    rights = [zero] * (count - 1) + [right]
    step = 1
    while step < count:
        w = []
        for j in range(count):
            total = ground[j]
            if j >= step:
                total = total + links[j - step]
            if j + step < count:
                total = total + links[j]
            w.append(1.0 / total)
        new_ground, new_r = list(ground), list(r)
        new_left, new_right = list(lefts), list(rights)
        new_links = [None] * count
        for j in range(count):
            if j >= step:
                al = links[j - step] * w[j - step]
                new_ground[j] = new_ground[j] + al * ground[j - step]
                new_r[j] = new_r[j] + al * r[j - step]
                if j - step < step:
                    new_left[j] = new_left[j] + al * lefts[j - step]
                if j >= 2 * step:
                    new_links[j - 2 * step] = al * links[j - 2 * step]
            if j + step < count:
                ga = links[j] * w[j + step]
                new_ground[j] = new_ground[j] + ga * ground[j + step]
                new_r[j] = new_r[j] + ga * r[j + step]
                if j + step >= count - step:
                    new_right[j] = new_right[j] + ga * rights[j + step]
        ground, r, lefts, rights, links = new_ground, new_r, new_left, new_right, new_links
        step *= 2
    w = [1.0 / g for g in ground]
    return [[a * b for a, b in zip(v, w)] for v in (r, lefts, rights)]


def apply_level(r, al, ga, step, axis):
    size = r.shape[axis]
    return r + al * pltpu.roll(r, step, axis) + ga * pltpu.roll(r, size - step, axis)


def half_coefs(a1, a2, b1, b2):
    out = [(None, None, a2[0], b2[0])]
    for i in range(1, len(a1)):
        e1 = out[-1][3]
        c = 1.0 / (1.0 - a1[i] * e1)
        be = b1[i] * e1
        f2 = c * a2[i]
        out.append((c, be, f2, be * f2 + b2[i]))
    return out


def half_values(a0, b0, a1, b1, coefs):
    out = [(a0[0], b0[0])]
    for i in range(1, len(a0)):
        c, be, _, _ = coefs[i]
        e0 = out[-1][1]
        f0 = c * (a0[i] + a1[i] * e0)
        out.append((f0, b0[i] + b1[i] * e0 + be * f0))
    return out


def half_back(values, coefs, beyond):
    first, last = [], []
    for (f0, e0), (_, _, f2, e1) in zip(reversed(values), reversed(coefs)):
        last.append(e0 + e1 * beyond)
        beyond = f0 + f2 * beyond
        first.append(beyond)
    return first[::-1], last[::-1]


def chain_coefs(a1, a2, b1, b2):
    m = len(a1) // 2
    low = half_coefs(a1[:m], a2[:m], b1[:m], b2[:m])
    high = half_coefs(b2[m:][::-1], b1[m:][::-1], a2[m:][::-1], a1[m:][::-1])
    return low, high, 1.0 / (1.0 - low[-1][3] * high[-1][3])


def chain_values(a0, b0, a1, a2, b1, b2, coefs):
    m = len(a0) // 2
    low, high, c = coefs
    low_values = half_values(a0[:m], b0[:m], a1[:m], b1[:m], low)
    high_values = half_values(b0[m:][::-1], a0[m:][::-1], b2[m:][::-1], a2[m:][::-1], high)
    low_end, high_end = low_values[-1][1], high_values[-1][1]
    end = c * (low_end + low[-1][3] * high_end)
    start = high_end + high[-1][3] * end
    first, last = half_back(low_values, low, start)
    last_high, first_high = half_back(high_values, high, end)
    return first + first_high[::-1], last + last_high[::-1]


def kernel(
    n, nw, x_hbm, zones_hbm, coef_hbm, out_ref,
    coef_ref, x_ref, zones_ref, T, K, S, U, SX, WL, WR, Y, PP, Q, AL, GA, WW, WP, WQ, DX, D, M, V,
    RL, RH, rows_out, rows_lo, rows_hi, cols_out, cols_lo, cols_hi,
    cs, cr, xs, xr, wc, wv,
    in_sem, halo_send, halo_recv, a_send, a_recv, b_send, b_recv, c_send, c_recv, d_send, d_recv,
):
    depth, rows, lanes = x_ref.shape
    pz = depth // n
    bz = SX.shape[2]
    nb = depth // bz
    per = bz // pz
    me = lax.axis_index("cast")
    mw = lax.axis_index("width")
    f32 = jnp.float32

    x_copy = pltpu.make_async_copy(x_hbm, x_ref, in_sem.at[0])
    zones_copy = pltpu.make_async_copy(zones_hbm, zones_ref, in_sem.at[1])
    coef_copy = pltpu.make_async_copy(coef_hbm, coef_ref, in_sem.at[2])
    x_copy.start()
    zones_copy.start()
    coef_copy.start()

    barrier = pltpu.get_barrier_semaphore()
    for k in range(1, n):
        pl.semaphore_signal(barrier, inc=1, device_id={"cast": lax.rem(me + k, n)})
    for k in range(1, nw):
        pl.semaphore_signal(barrier, inc=1, device_id={"width": lax.rem(mw + k, nw)})

    lane2 = lax.broadcasted_iota(jnp.int32, (bz, lanes), 1)
    zero = jnp.zeros((bz, lanes), f32)
    cast_lo = (me > 0).astype(f32)
    cast_hi = (me < n - 1).astype(f32)
    width_lo = (mw > 0).astype(f32)
    width_hi = (mw < nw - 1).astype(f32)

    def pack(v, b):
        acc = zero
        for j in range(rows):
            acc = jnp.where(lane2 // 2 == j, pltpu.roll(v[j], 2 * j + 1, 1), acc)
        return acc if isinstance(b, int) and b == 0 else pltpu.roll(acc, b * (2 * rows), 1)

    def spread(p, b, odd):
        q = pltpu.roll(p, lax.rem(lanes - b * (2 * rows), lanes), 1)
        return [
            jnp.broadcast_to(q[:, 2 * j + odd : 2 * j + odd + 1], (bz, lanes))
            for j in range(rows)
        ]

    def by_rows(ref, start):
        return [ref[pl.ds(start, bz), j, :] for j in range(rows)]

    x_copy.wait()
    rows_out[0] = x_ref[:, 0, :]
    rows_out[1] = x_ref[:, rows - 1, :]
    cols_out[...] = lax.fori_loop(
        0, nb, lambda b, acc: acc + pack(by_rows(x_ref, b * bz), b), zero
    )

    @pl.when(me == 0)
    def _():
        rows_lo[...] = jnp.zeros_like(rows_lo)

    @pl.when(me == n - 1)
    def _():
        rows_hi[...] = jnp.zeros_like(rows_hi)

    @pl.when(mw == 0)
    def _():
        cols_lo[...] = jnp.zeros_like(cols_lo)

    @pl.when(mw == nw - 1)
    def _():
        cols_hi[...] = jnp.zeros_like(cols_hi)

    def remote(src, dst, send, recv, device):
        return pltpu.make_async_remote_copy(
            src_ref=src, dst_ref=dst, send_sem=send, recv_sem=recv,
            device_id=device, device_id_type=pl.DeviceIdType.MESH,
        )

    halos = [
        (remote(rows_out.at[1], rows_lo, halo_send.at[0], halo_recv.at[0],
                {"cast": lax.rem(me + 1, n)}), me < n - 1, me > 0),
        (remote(rows_out.at[0], rows_hi, halo_send.at[1], halo_recv.at[1],
                {"cast": lax.rem(me + n - 1, n)}), me > 0, me < n - 1),
        (remote(cols_out, cols_lo, halo_send.at[2], halo_recv.at[2],
                {"width": lax.rem(mw + 1, nw)}), mw < nw - 1, mw > 0),
        (remote(cols_out, cols_hi, halo_send.at[3], halo_recv.at[3],
                {"width": lax.rem(mw + nw - 1, nw)}), mw > 0, mw < nw - 1),
    ]
    pl.semaphore_wait(barrier, n - 1 + nw - 1)
    for copy, sends, _ in halos:
        pl.when(sends)(copy.start)

    def properties(b, _):
        z = pl.ds(b * bz, bz)
        t, hot, cond = medium(x_ref[z])
        T[pl.ds(b * bz + 1, bz)] = hot
        K[pl.ds(b * bz + 1, bz)] = cond
        S[z] = 1.0 / ((1.0 - RELEASE) + RELEASE * t * t)
        U[z] = jnp.zeros((bz, rows, lanes), f32)
        for j, v in enumerate(by_rows(S, b * bz)):
            SX[b, j] = v
        return 0

    lax.fori_loop(0, nb, properties, 0)
    T[0], T[depth + 1] = T[1], T[depth]
    K[0], K[depth + 1] = -K[1], -K[depth]
    zones_copy.wait()
    coef_copy.wait()
    for side, plane in ((0, 0), (1, depth - 1)):
        zone = zones_ref[side]
        coef = jnp.zeros((rows, lanes), f32)
        for i in range(coef_ref.shape[0]):
            coef = jnp.where(zone == i, coef_ref[i], coef)
        U[plane] = coef * (depth * depth / 8.0)

    for copy, _, receives in halos:
        pl.when(receives)(copy.wait_recv)

    gain_cast = rows * rows * 4.0 * 0.5
    gain_width = lanes * lanes / 4.0 * 0.5
    gain_thick = depth * depth / 4.0 * 0.5
    width_lo_mask = jnp.where(lane2 == 0, width_lo, 1.0)
    width_hi_mask = jnp.where(lane2 == lanes - 1, width_hi, 1.0)
    _, col_lo_T, col_lo_K = medium(cols_lo[...])
    _, col_hi_T, col_hi_K = medium(cols_hi[...])

    def gather_copy(dest):
        return remote(cs.at[dest], cr.at[me], a_send.at[dest], a_recv.at[me], {"cast": dest})

    def gather_wait(source):
        remote(cs.at[source], cr.at[source], a_send.at[source], a_recv.at[source],
               {"cast": source}).wait_recv()

    def cast_block(k, _):
        b = lax.rem(me // per + nb // 2 + k, nb)
        start = pl.multiple_of(b * bz, bz)
        hot, cond = by_rows(T, start + 1), by_rows(K, start + 1)
        hot_m, cond_m = by_rows(T, start), by_rows(K, start)
        hot_p, cond_p = by_rows(T, start + 2), by_rows(K, start + 2)
        surf = by_rows(U, start)
        _, hot_lo, cond_lo = medium(rows_lo[pl.ds(start, bz), :])
        _, hot_hi, cond_hi = medium(rows_hi[pl.ds(start, bz), :])
        hots, conds = [hot_lo] + hot + [hot_hi], [cond_lo] + cond + [cond_hi]
        faces = [gain_cast * (conds[j] + conds[j + 1]) for j in range(rows + 1)]
        root_lo, root_hi = jnp.sqrt(faces[0]), jnp.sqrt(faces[rows])
        inv_lo, inv_hi = 1.0 / root_lo, 1.0 / root_hi
        RL[b], RH[b] = inv_lo, inv_hi
        faces[0], faces[rows] = faces[0] * cast_lo, faces[rows] * cast_hi
        flux = [faces[j] * (hots[j + 1] - hots[j]) for j in range(rows + 1)]

        lo_T, lo_K = spread(col_lo_T, b, 0), spread(col_lo_K, b, 0)
        hi_T, hi_K = spread(col_hi_T, b, 1), spread(col_hi_K, b, 1)
        r = []
        for j in range(rows):
            h, c = hot[j], cond[j]
            hm = jnp.where(lane2 == 0, lo_T[j], pltpu.roll(h, 1, 1))
            cm = jnp.where(lane2 == 0, lo_K[j], pltpu.roll(c, 1, 1))
            hp = jnp.where(lane2 == lanes - 1, hi_T[j], pltpu.roll(h, lanes - 1, 1))
            cp = jnp.where(lane2 == lanes - 1, hi_K[j], pltpu.roll(c, lanes - 1, 1))
            lo = gain_width * (c + cm) * width_lo_mask
            hi = gain_width * (c + cp) * width_hi_mask
            WL[b, j] = lo
            WR[b, j] = hi
            r.append(
                surf[j] * (MEDIUM - h)
                + (flux[j + 1] - flux[j])
                + (hi * (hp - h) - lo * (h - hm))
                + gain_thick
                * ((c + cond_p[j]) * (hot_p[j] - h) - (c + cond_m[j]) * (h - hot_m[j]))
            )
        s = [SX[b, j] for j in range(rows)]
        ys, ps, qs = row_levels(s, faces[1:rows], faces[0], faces[rows], r)
        for j in range(rows):
            Y[b, j] = ys[j]
            PP[b, j] = ps[j]
            Q[b, j] = qs[j]
        cross = jnp.where(
            me == n - 1, ps[-1] * (root_hi * inv_lo), qs[0] * (root_lo * inv_hi)
        )
        sent = (ys[0] * root_lo, ps[0], cross, ys[-1] * root_hi, qs[-1])
        for o in range(per):
            dest = b * per + o
            for v, value in enumerate(sent):
                cs[dest, v * pz : (v + 1) * pz] = value[o * pz : (o + 1) * pz]

            @pl.when(dest != me)
            def _():
                gather_copy(dest).start()

        return 0

    lax.fori_loop(0, nb, cast_block, 0)
    cr[me] = cs[me]

    lane4 = lax.broadcasted_iota(jnp.int32, SX.shape, 3)
    lo, hi = WL[...], WR[...]
    left = jnp.where(lane4 == 0, lo, 0.0)
    right = jnp.where(lane4 == lanes - 1, hi, 0.0)
    ground, left, right, factors = lane_levels(
        SX[...] + left + right, lo - left, hi - right, left, right
    )
    for i, (al, ga) in enumerate(factors):
        AL[i] = al
        GA[i] = ga
    w = 1.0 / ground
    p, q = left * w, right * w
    WW[...], WP[...], WQ[...] = w, p, q
    p_ends = sum(pack(p[b], b) for b in range(nb))
    q_ends = sum(pack(q[b], b) for b in range(nb))
    wc[mw, 0] = p_ends
    wc[mw, 1] = q_ends
    wide_coefs = [
        remote(wc.at[mw], wc.at[mw], c_send.at[k - 1], c_recv.at[k - 1],
               {"width": lax.rem(mw + k, nw)})
        for k in range(1, nw)
    ]
    for copy in wide_coefs:
        copy.start()

    for i in range(n):
        pl.when(me != i)(functools.partial(gather_wait, i))
    got = [[cr[i, v * pz : (v + 1) * pz] for v in range(5)] for i in range(n)]
    a0, a1, a2, b0, b2 = [[got[i][v] for i in range(n)] for v in range(5)]
    b1 = a2
    first, last = chain_values(
        a0, b0, a1, a2, b1, b2, chain_coefs(a1, a2, b1, b2)
    )
    blank = jnp.zeros_like(first[0])

    def answer_copy(i):
        return remote(xs.at[i], xr.at[me], b_send.at[i], b_recv.at[me], {"cast": i})

    for i in range(n):
        xs[i, 0:pz] = last[i - 1] if i > 0 else blank
        xs[i, pz : 2 * pz] = first[i + 1] if i < n - 1 else blank
        pl.when(me != i)(answer_copy(i).start)
    xr[me] = xs[me]

    half = depth // 2
    zlo_sum, zhi_sum = S[0] + U[0], S[depth - 1] + U[depth - 1]
    for i in range(half - 1):
        j = depth - 1 - i
        glo, ghi = gain_thick * (K[i + 1] + K[i + 2]), gain_thick * (K[j] + K[j + 1])
        wlo, whi = 1.0 / (zlo_sum + glo), 1.0 / (zhi_sum + ghi)
        mlo, mhi = glo * wlo, ghi * whi
        M[i], M[j] = mlo, mhi
        V[i], V[j] = wlo, whi
        zlo_sum = S[i + 1] + mlo * zlo_sum
        zhi_sum = S[j - 1] + mhi * zhi_sum
    gmid = gain_thick * (K[half] + K[half + 1])
    det = 1.0 / (zlo_sum * zhi_sum + gmid * (zlo_sum + zhi_sum))
    V[half - 1] = (zhi_sum + gmid) * det
    V[half] = (zlo_sum + gmid) * det
    M[half] = gmid * det

    def answer_wait(i):
        remote(xs.at[i], xr.at[i], b_send.at[i], b_recv.at[i], {"cast": i}).wait_recv()

    for i in range(n):
        pl.when(me != i)(functools.partial(answer_wait, i))
    los = jnp.concatenate([xr[i, 0:pz] for i in range(n)], 0).reshape(nb, bz, lanes)
    his = jnp.concatenate([xr[i, pz : 2 * pz] for i in range(n)], 0).reshape(nb, bz, lanes)
    los, his = (los * RL[...])[:, None], (his * RH[...])[:, None]
    r = (Y[...] + PP[...] * los + Q[...] * his) * SX[...]
    step, i = 1, 0
    while step < lanes:
        r = apply_level(r, AL[i], GA[i], step, 3)
        step, i = step * 2, i + 1
    r = r * WW[...]
    DX[...] = r
    wv[mw] = sum(pack(r[b], b) for b in range(nb))
    wide_values = [
        remote(wv.at[mw], wv.at[mw], d_send.at[k - 1], d_recv.at[k - 1],
               {"width": lax.rem(mw + k, nw)})
        for k in range(1, nw)
    ]
    for copy in wide_values:
        copy.start()

    for copy in wide_coefs:
        copy.wait_recv()

    def firsts(p):
        return pltpu.roll(p, lanes - 1, 1)

    even = lane2 % 2 == 0
    b1 = [jnp.where(even, wc[i, 0], 0.0) for i in range(nw)]
    b2 = [jnp.where(even, wc[i, 1], 0.0) for i in range(nw)]
    a1 = [jnp.where(even, firsts(wc[i, 0]), 0.0) for i in range(nw)]
    a2 = [jnp.where(even, firsts(wc[i, 1]), 0.0) for i in range(nw)]
    coefs = chain_coefs(a1, a2, b1, b2)
    for copy in wide_values:
        copy.wait_recv()
    b0 = [wv[i] for i in range(nw)]
    a0 = [firsts(b0[i]) for i in range(nw)]
    first, last = chain_values(a0, b0, a1, a2, b1, b2, coefs)
    before, after = zero, zero
    for i in range(nw):
        if i > 0:
            before = jnp.where(mw == i, last[i - 1], before)
        if i < nw - 1:
            after = jnp.where(mw == i, first[i + 1], after)

    def thick_block(b, _):
        start = b * bz
        los, his = spread(before, b, 0), spread(after, b, 0)
        for j in range(rows):
            D[pl.ds(start, bz), j, :] = (DX[b, j] + WP[b, j] * los[j] + WQ[b, j] * his[j]) * SX[
                b, j
            ]
        return 0

    lax.fori_loop(0, nb, thick_block, 0)

    dlo, dhi = D[0], D[depth - 1]
    for i in range(half - 1):
        j = depth - 1 - i
        D[i], D[j] = dlo, dhi
        dlo = D[i + 1] + M[i] * dlo
        dhi = D[j - 1] + M[j] * dhi
    ulo = V[half - 1] * dlo + M[half] * dhi
    uhi = V[half] * dhi + M[half] * dlo
    out_ref[half - 1] = ulo * S[half - 1]
    out_ref[half] = uhi * S[half]
    for i in range(half - 2, -1, -1):
        j = depth - 1 - i
        ulo = V[i] * D[i] + M[i] * ulo
        uhi = V[j] * D[j] + M[j] * uhi
        out_ref[i] = ulo * S[i]
        out_ref[j] = uhi * S[j]

    for copy, sends, _ in halos:
        pl.when(sends)(copy.wait_send)
    for i in range(n):
        pl.when(me != i)(gather_copy(i).wait_send)
    for i in range(n):
        pl.when(me != i)(answer_copy(i).wait_send)
    for copy in wide_coefs + wide_values:
        copy.wait_send()


def shards(n, nw, x, zones, spray_coef):
    depth, rows, lanes = x.shape
    pz = depth // n
    f32 = jnp.float32
    vmem = pltpu.VMEM
    bz = max(pz, depth // 2)
    nb = depth // bz
    field = vmem((depth, rows, lanes), f32)
    blocks = vmem((nb, rows, bz, lanes), f32)
    padded = vmem((depth + 2, rows, lanes), f32)
    levels = vmem(((lanes - 1).bit_length(), nb, rows, bz, lanes), f32)
    edge = vmem((depth, lanes), f32)
    packed = vmem((bz, lanes), f32)
    dma = pltpu.SemaphoreType.DMA
    scratch = (
        [pltpu.SMEM(spray_coef.shape, f32)]
        + [field, vmem(zones.shape, zones.dtype), padded, padded]
        + [field, field]
        + [blocks] * 6
        + [levels, levels]
        + [blocks] * 4
        + [field] * 3
        + [vmem((nb, bz, lanes), f32)] * 2
        + [vmem((2, depth, lanes), f32), edge, edge, packed, packed, packed]
        + [
            vmem((n, 5 * pz, lanes), f32),
            vmem((n, 5 * pz, lanes), f32),
            vmem((n, 2 * pz, lanes), f32),
            vmem((n, 2 * pz, lanes), f32),
            vmem((nw, 2, bz, lanes), f32),
            vmem((nw, bz, lanes), f32),
        ]
        + [dma((3,)), dma((4,)), dma((4,))]
        + [dma((n,))] * 4
        + [dma((nw,))] * 4
    )
    step = pl.pallas_call(
        functools.partial(kernel, n, nw),
        out_shape=jax.ShapeDtypeStruct(x.shape, f32),
        in_specs=[
            pl.BlockSpec(memory_space=pltpu.HBM),
            pl.BlockSpec(memory_space=pltpu.HBM),
            pl.BlockSpec(memory_space=pltpu.HBM),
        ],
        out_specs=pl.BlockSpec(memory_space=pltpu.VMEM),
        scratch_shapes=scratch,
        compiler_params=pltpu.CompilerParams(
            collective_id=0, has_side_effects=True, vmem_limit_bytes=63 * 1024 * 1024
        ),
        cost_estimate=pl.CostEstimate(
            flops=20_000_000, bytes_accessed=1_000_000, transcendentals=100_000
        ),
        name="adi_step",
    )(x, zones, spray_coef)
    return x + step


def solution(mesh):
    spec = P(None, "cast", "width")
    body = functools.partial(shards, mesh.shape["cast"], mesh.shape["width"])
    return jax.shard_map(
        body, mesh=mesh, in_specs=(spec, spec, P()), out_specs=spec, check_vma=False
    )
```

```python
import functools

import jax
import jax.numpy as jnp
from jax import lax
from jax.experimental import pallas as pl
from jax.experimental.pallas import tpu as pltpu
from jax.sharding import PartitionSpec as P

RELEASE = 0.4
MEDIUM = -2.0


def medium(x):
    t = jnp.tanh(x)
    hot = x - RELEASE * t
    cond = 1.5 - 0.5 * jnp.tanh(hot)
    return t, hot, cond


def lane_levels(ground, gl, gr, left, right):
    axis = ground.ndim - 1
    size = ground.shape[axis]
    lane = lax.broadcasted_iota(jnp.int32, ground.shape, axis)
    ends = left + right
    factors = []
    step = 1
    while step < size:
        w = 1.0 / (ground + gl + gr)
        al = gl * pltpu.roll(w, step, axis)
        ga = gr * pltpu.roll(w, size - step, axis)
        factors.append((al, ga))
        ground = (
            ground
            + al * pltpu.roll(ground, step, axis)
            + ga * pltpu.roll(ground, size - step, axis)
        )
        from_left = al * pltpu.roll(ends, step, axis)
        from_right = ga * pltpu.roll(ends, size - step, axis)
        if 2 * step < size:
            ends = ends + from_left + from_right
            gl = al * pltpu.roll(gl, step, axis)
            gr = ga * pltpu.roll(gr, size - step, axis)
        else:
            left = jnp.where(lane < step, ends, 0.0) + from_left
            right = jnp.where(lane >= step, ends, 0.0) + from_right
        step *= 2
    return ground, left, right, factors


def row_levels(ground, links, left, right, r):
    count = len(ground)
    zero = jnp.zeros_like(left)
    ground = list(ground)
    ground[0] = ground[0] + left
    ground[-1] = ground[-1] + right
    lefts = [left] + [zero] * (count - 1)
    rights = [zero] * (count - 1) + [right]
    step = 1
    while step < count:
        w = []
        for j in range(count):
            total = ground[j]
            if j >= step:
                total = total + links[j - step]
            if j + step < count:
                total = total + links[j]
            w.append(1.0 / total)
        new_ground, new_r = list(ground), list(r)
        new_left, new_right = list(lefts), list(rights)
        new_links = [None] * count
        for j in range(count):
            if j >= step:
                al = links[j - step] * w[j - step]
                new_ground[j] = new_ground[j] + al * ground[j - step]
                new_r[j] = new_r[j] + al * r[j - step]
                if j - step < step:
                    new_left[j] = new_left[j] + al * lefts[j - step]
                if j >= 2 * step:
                    new_links[j - 2 * step] = al * links[j - 2 * step]
            if j + step < count:
                ga = links[j] * w[j + step]
                new_ground[j] = new_ground[j] + ga * ground[j + step]
                new_r[j] = new_r[j] + ga * r[j + step]
                if j + step >= count - step:
                    new_right[j] = new_right[j] + ga * rights[j + step]
        ground, r, lefts, rights, links = new_ground, new_r, new_left, new_right, new_links
        step *= 2
    w = [1.0 / g for g in ground]
    return [[a * b for a, b in zip(v, w)] for v in (r, lefts, rights)]


def apply_level(r, al, ga, step, axis):
    size = r.shape[axis]
    return r + al * pltpu.roll(r, step, axis) + ga * pltpu.roll(r, size - step, axis)


def half_coefs(a1, a2, b1, b2):
    out = [(None, None, a2[0], b2[0])]
    for i in range(1, len(a1)):
        e1 = out[-1][3]
        c = 1.0 / (1.0 - a1[i] * e1)
        be = b1[i] * e1
        f2 = c * a2[i]
        out.append((c, be, f2, be * f2 + b2[i]))
    return out


def half_values(a0, b0, a1, b1, coefs):
    out = [(a0[0], b0[0])]
    for i in range(1, len(a0)):
        c, be, _, _ = coefs[i]
        e0 = out[-1][1]
        f0 = c * (a0[i] + a1[i] * e0)
        out.append((f0, b0[i] + b1[i] * e0 + be * f0))
    return out


def half_back(values, coefs, beyond):
    first, last = [], []
    for (f0, e0), (_, _, f2, e1) in zip(reversed(values), reversed(coefs)):
        last.append(e0 + e1 * beyond)
        beyond = f0 + f2 * beyond
        first.append(beyond)
    return first[::-1], last[::-1]


def chain_coefs(a1, a2, b1, b2):
    m = len(a1) // 2
    low = half_coefs(a1[:m], a2[:m], b1[:m], b2[:m])
    high = half_coefs(b2[m:][::-1], b1[m:][::-1], a2[m:][::-1], a1[m:][::-1])
    return low, high, 1.0 / (1.0 - low[-1][3] * high[-1][3])


def chain_values(a0, b0, a1, a2, b1, b2, coefs):
    m = len(a0) // 2
    low, high, c = coefs
    low_values = half_values(a0[:m], b0[:m], a1[:m], b1[:m], low)
    high_values = half_values(b0[m:][::-1], a0[m:][::-1], b2[m:][::-1], a2[m:][::-1], high)
    low_end, high_end = low_values[-1][1], high_values[-1][1]
    end = c * (low_end + low[-1][3] * high_end)
    start = high_end + high[-1][3] * end
    first, last = half_back(low_values, low, start)
    last_high, first_high = half_back(high_values, high, end)
    return first + first_high[::-1], last + last_high[::-1]


def kernel(
    n, nw, x_hbm, zones_hbm, coef_hbm, out_ref,
    coef_ref, x_ref, zones_ref, T, K, S, U, SX, WL, WR, Y, PP, Q, AL, GA, WW, WP, WQ, DX, D, M, V, O,
    RL, RH, rows_out, rows_lo, rows_hi, cols_out, cols_lo, cols_hi,
    cs, cr, xs, xr, wc, wv,
    in_sem, out_sem, halo_send, halo_recv, a_send, a_recv, b_send, b_recv, c_send, c_recv, d_send, d_recv,
):
    depth, rows, lanes = x_ref.shape
    pz = depth // n
    bz = SX.shape[2]
    nb = depth // bz
    per = bz // pz
    me = lax.axis_index("cast")
    mw = lax.axis_index("width")
    f32 = jnp.float32

    x_copy = pltpu.make_async_copy(x_hbm, x_ref, in_sem.at[0])
    zones_copy = pltpu.make_async_copy(zones_hbm, zones_ref, in_sem.at[1])
    coef_copy = pltpu.make_async_copy(coef_hbm, coef_ref, in_sem.at[2])
    x_copy.start()
    zones_copy.start()
    coef_copy.start()

    barrier = pltpu.get_barrier_semaphore()
    for k in range(1, n):
        pl.semaphore_signal(barrier, inc=1, device_id={"cast": lax.rem(me + k, n)})
    for k in range(1, nw):
        pl.semaphore_signal(barrier, inc=1, device_id={"width": lax.rem(mw + k, nw)})

    lane2 = lax.broadcasted_iota(jnp.int32, (bz, lanes), 1)
    zero = jnp.zeros((bz, lanes), f32)
    cast_lo = (me > 0).astype(f32)
    cast_hi = (me < n - 1).astype(f32)
    width_lo = (mw > 0).astype(f32)
    width_hi = (mw < nw - 1).astype(f32)

    def pack(v, b):
        acc = zero
        for j in range(rows):
            acc = jnp.where(lane2 // 2 == j, pltpu.roll(v[j], 2 * j + 1, 1), acc)
        return acc if isinstance(b, int) and b == 0 else pltpu.roll(acc, b * (2 * rows), 1)

    def spread(p, b, odd):
        q = pltpu.roll(p, lax.rem(lanes - b * (2 * rows), lanes), 1)
        return [
            jnp.broadcast_to(q[:, 2 * j + odd : 2 * j + odd + 1], (bz, lanes))
            for j in range(rows)
        ]

    def by_rows(ref, start):
        return [ref[pl.ds(start, bz), j, :] for j in range(rows)]

    x_copy.wait()
    rows_out[0] = x_ref[:, 0, :]
    rows_out[1] = x_ref[:, rows - 1, :]
    cols_out[...] = lax.fori_loop(
        0, nb, lambda b, acc: acc + pack(by_rows(x_ref, b * bz), b), zero
    )

    @pl.when(me == 0)
    def _():
        rows_lo[...] = jnp.zeros_like(rows_lo)

    @pl.when(me == n - 1)
    def _():
        rows_hi[...] = jnp.zeros_like(rows_hi)

    @pl.when(mw == 0)
    def _():
        cols_lo[...] = jnp.zeros_like(cols_lo)

    @pl.when(mw == nw - 1)
    def _():
        cols_hi[...] = jnp.zeros_like(cols_hi)

    def remote(src, dst, send, recv, device):
        return pltpu.make_async_remote_copy(
            src_ref=src, dst_ref=dst, send_sem=send, recv_sem=recv,
            device_id=device, device_id_type=pl.DeviceIdType.MESH,
        )

    halos = [
        (remote(rows_out.at[1], rows_lo, halo_send.at[0], halo_recv.at[0],
                {"cast": lax.rem(me + 1, n)}), me < n - 1, me > 0),
        (remote(rows_out.at[0], rows_hi, halo_send.at[1], halo_recv.at[1],
                {"cast": lax.rem(me + n - 1, n)}), me > 0, me < n - 1),
        (remote(cols_out, cols_lo, halo_send.at[2], halo_recv.at[2],
                {"width": lax.rem(mw + 1, nw)}), mw < nw - 1, mw > 0),
        (remote(cols_out, cols_hi, halo_send.at[3], halo_recv.at[3],
                {"width": lax.rem(mw + nw - 1, nw)}), mw > 0, mw < nw - 1),
    ]
    pl.semaphore_wait(barrier, n - 1 + nw - 1)
    for copy, sends, _ in halos:
        pl.when(sends)(copy.start)

    def properties(b, _):
        z = pl.ds(b * bz, bz)
        t, hot, cond = medium(x_ref[z])
        T[pl.ds(b * bz + 1, bz)] = hot
        K[pl.ds(b * bz + 1, bz)] = cond
        S[z] = 1.0 / ((1.0 - RELEASE) + RELEASE * t * t)
        U[z] = jnp.zeros((bz, rows, lanes), f32)
        for j, v in enumerate(by_rows(S, b * bz)):
            SX[b, j] = v
        return 0

    lax.fori_loop(0, nb, properties, 0)
    T[0], T[depth + 1] = T[1], T[depth]
    K[0], K[depth + 1] = -K[1], -K[depth]
    zones_copy.wait()
    coef_copy.wait()
    for side, plane in ((0, 0), (1, depth - 1)):
        zone = zones_ref[side]
        coef = jnp.zeros((rows, lanes), f32)
        for i in range(coef_ref.shape[0]):
            coef = jnp.where(zone == i, coef_ref[i], coef)
        U[plane] = coef * (depth * depth / 8.0)

    for copy, _, receives in halos:
        pl.when(receives)(copy.wait_recv)

    gain_cast = rows * rows * 4.0 * 0.5
    gain_width = lanes * lanes / 4.0 * 0.5
    gain_thick = depth * depth / 4.0 * 0.5
    width_lo_mask = jnp.where(lane2 == 0, width_lo, 1.0)
    width_hi_mask = jnp.where(lane2 == lanes - 1, width_hi, 1.0)
    _, col_lo_T, col_lo_K = medium(cols_lo[...])
    _, col_hi_T, col_hi_K = medium(cols_hi[...])

    def gather_copy(dest):
        return remote(cs.at[dest], cr.at[me], a_send.at[dest], a_recv.at[me], {"cast": dest})

    def gather_wait(source):
        remote(cs.at[source], cr.at[source], a_send.at[source], a_recv.at[source],
               {"cast": source}).wait_recv()

    def cast_block(k, _):
        b = lax.rem(me // per + nb // 2 + k, nb)
        start = pl.multiple_of(b * bz, bz)
        hot, cond = by_rows(T, start + 1), by_rows(K, start + 1)
        hot_m, cond_m = by_rows(T, start), by_rows(K, start)
        hot_p, cond_p = by_rows(T, start + 2), by_rows(K, start + 2)
        surf = by_rows(U, start)
        _, hot_lo, cond_lo = medium(rows_lo[pl.ds(start, bz), :])
        _, hot_hi, cond_hi = medium(rows_hi[pl.ds(start, bz), :])
        hots, conds = [hot_lo] + hot + [hot_hi], [cond_lo] + cond + [cond_hi]
        faces = [gain_cast * (conds[j] + conds[j + 1]) for j in range(rows + 1)]
        root_lo, root_hi = jnp.sqrt(faces[0]), jnp.sqrt(faces[rows])
        inv_lo, inv_hi = 1.0 / root_lo, 1.0 / root_hi
        RL[b], RH[b] = inv_lo, inv_hi
        faces[0], faces[rows] = faces[0] * cast_lo, faces[rows] * cast_hi
        flux = [faces[j] * (hots[j + 1] - hots[j]) for j in range(rows + 1)]

        lo_T, lo_K = spread(col_lo_T, b, 0), spread(col_lo_K, b, 0)
        hi_T, hi_K = spread(col_hi_T, b, 1), spread(col_hi_K, b, 1)
        r = []
        for j in range(rows):
            h, c = hot[j], cond[j]
            hm = jnp.where(lane2 == 0, lo_T[j], pltpu.roll(h, 1, 1))
            cm = jnp.where(lane2 == 0, lo_K[j], pltpu.roll(c, 1, 1))
            hp = jnp.where(lane2 == lanes - 1, hi_T[j], pltpu.roll(h, lanes - 1, 1))
            cp = jnp.where(lane2 == lanes - 1, hi_K[j], pltpu.roll(c, lanes - 1, 1))
            lo = gain_width * (c + cm) * width_lo_mask
            hi = gain_width * (c + cp) * width_hi_mask
            WL[b, j] = lo
            WR[b, j] = hi
            r.append(
                surf[j] * (MEDIUM - h)
                + (flux[j + 1] - flux[j])
                + (hi * (hp - h) - lo * (h - hm))
                + gain_thick
                * ((c + cond_p[j]) * (hot_p[j] - h) - (c + cond_m[j]) * (h - hot_m[j]))
            )
        s = [SX[b, j] for j in range(rows)]
        ys, ps, qs = row_levels(s, faces[1:rows], faces[0], faces[rows], r)
        for j in range(rows):
            Y[b, j] = ys[j]
            PP[b, j] = ps[j]
            Q[b, j] = qs[j]
        cross = jnp.where(
            me == n - 1, ps[-1] * (root_hi * inv_lo), qs[0] * (root_lo * inv_hi)
        )
        sent = (ys[0] * root_lo, ps[0], cross, ys[-1] * root_hi, qs[-1])
        for o in range(per):
            dest = b * per + o
            for v, value in enumerate(sent):
                cs[dest, v * pz : (v + 1) * pz] = value[o * pz : (o + 1) * pz]

            @pl.when(dest != me)
            def _():
                gather_copy(dest).start()

        return 0

    lax.fori_loop(0, nb, cast_block, 0)
    cr[me] = cs[me]

    lane4 = lax.broadcasted_iota(jnp.int32, SX.shape, 3)
    lo, hi = WL[...], WR[...]
    left = jnp.where(lane4 == 0, lo, 0.0)
    right = jnp.where(lane4 == lanes - 1, hi, 0.0)
    ground, left, right, factors = lane_levels(
        SX[...] + left + right, lo - left, hi - right, left, right
    )
    for i, (al, ga) in enumerate(factors):
        AL[i] = al
        GA[i] = ga
    w = 1.0 / ground
    p, q = left * w, right * w
    WW[...], WP[...], WQ[...] = w, p, q
    p_ends = sum(pack(p[b], b) for b in range(nb))
    q_ends = sum(pack(q[b], b) for b in range(nb))
    wc[mw, 0] = p_ends
    wc[mw, 1] = q_ends
    wide_coefs = [
        remote(wc.at[mw], wc.at[mw], c_send.at[k - 1], c_recv.at[k - 1],
               {"width": lax.rem(mw + k, nw)})
        for k in range(1, nw)
    ]
    for copy in wide_coefs:
        copy.start()

    for i in range(n):
        pl.when(me != i)(functools.partial(gather_wait, i))
    got = [[cr[i, v * pz : (v + 1) * pz] for v in range(5)] for i in range(n)]
    a0, a1, a2, b0, b2 = [[got[i][v] for i in range(n)] for v in range(5)]
    b1 = a2
    first, last = chain_values(
        a0, b0, a1, a2, b1, b2, chain_coefs(a1, a2, b1, b2)
    )
    blank = jnp.zeros_like(first[0])

    def answer_copy(i):
        return remote(xs.at[i], xr.at[me], b_send.at[i], b_recv.at[me], {"cast": i})

    for i in range(n):
        xs[i, 0:pz] = last[i - 1] if i > 0 else blank
        xs[i, pz : 2 * pz] = first[i + 1] if i < n - 1 else blank
        pl.when(me != i)(answer_copy(i).start)
    xr[me] = xs[me]

    half = depth // 2
    zlo_sum, zhi_sum = S[0] + U[0], S[depth - 1] + U[depth - 1]
    for i in range(half - 1):
        j = depth - 1 - i
        glo, ghi = gain_thick * (K[i + 1] + K[i + 2]), gain_thick * (K[j] + K[j + 1])
        wlo, whi = 1.0 / (zlo_sum + glo), 1.0 / (zhi_sum + ghi)
        mlo, mhi = glo * wlo, ghi * whi
        M[i], M[j] = mlo, mhi
        V[i], V[j] = wlo, whi
        zlo_sum = S[i + 1] + mlo * zlo_sum
        zhi_sum = S[j - 1] + mhi * zhi_sum
    gmid = gain_thick * (K[half] + K[half + 1])
    det = 1.0 / (zlo_sum * zhi_sum + gmid * (zlo_sum + zhi_sum))
    V[half - 1] = (zhi_sum + gmid) * det
    V[half] = (zlo_sum + gmid) * det
    M[half] = gmid * det

    def answer_wait(i):
        remote(xs.at[i], xr.at[i], b_send.at[i], b_recv.at[i], {"cast": i}).wait_recv()

    for i in range(n):
        pl.when(me != i)(functools.partial(answer_wait, i))
    los = jnp.concatenate([xr[i, 0:pz] for i in range(n)], 0).reshape(nb, bz, lanes)
    his = jnp.concatenate([xr[i, pz : 2 * pz] for i in range(n)], 0).reshape(nb, bz, lanes)
    los, his = (los * RL[...])[:, None], (his * RH[...])[:, None]
    r = (Y[...] + PP[...] * los + Q[...] * his) * SX[...]
    step, i = 1, 0
    while step < lanes:
        r = apply_level(r, AL[i], GA[i], step, 3)
        step, i = step * 2, i + 1
    r = r * WW[...]
    DX[...] = r
    wv[mw] = sum(pack(r[b], b) for b in range(nb))
    wide_values = [
        remote(wv.at[mw], wv.at[mw], d_send.at[k - 1], d_recv.at[k - 1],
               {"width": lax.rem(mw + k, nw)})
        for k in range(1, nw)
    ]
    for copy in wide_values:
        copy.start()

    for copy in wide_coefs:
        copy.wait_recv()

    def firsts(p):
        return pltpu.roll(p, lanes - 1, 1)

    even = lane2 % 2 == 0
    b1 = [jnp.where(even, wc[i, 0], 0.0) for i in range(nw)]
    b2 = [jnp.where(even, wc[i, 1], 0.0) for i in range(nw)]
    a1 = [jnp.where(even, firsts(wc[i, 0]), 0.0) for i in range(nw)]
    a2 = [jnp.where(even, firsts(wc[i, 1]), 0.0) for i in range(nw)]
    coefs = chain_coefs(a1, a2, b1, b2)
    for copy in wide_values:
        copy.wait_recv()
    b0 = [wv[i] for i in range(nw)]
    a0 = [firsts(b0[i]) for i in range(nw)]
    first, last = chain_values(a0, b0, a1, a2, b1, b2, coefs)
    before, after = zero, zero
    for i in range(nw):
        if i > 0:
            before = jnp.where(mw == i, last[i - 1], before)
        if i < nw - 1:
            after = jnp.where(mw == i, first[i + 1], after)

    def thick_block(b, _):
        start = b * bz
        los, his = spread(before, b, 0), spread(after, b, 0)
        for j in range(rows):
            D[pl.ds(start, bz), j, :] = (DX[b, j] + WP[b, j] * los[j] + WQ[b, j] * his[j]) * SX[
                b, j
            ]
        return 0

    lax.fori_loop(0, nb, thick_block, 0)

    dlo, dhi = D[0], D[depth - 1]
    for i in range(half - 1):
        j = depth - 1 - i
        D[i], D[j] = dlo, dhi
        dlo = D[i + 1] + M[i] * dlo
        dhi = D[j - 1] + M[j] * dhi
    ulo = V[half - 1] * dlo + M[half] * dhi
    uhi = V[half] * dhi + M[half] * dlo
    O[half - 1] = ulo * S[half - 1]
    O[half] = uhi * S[half]
    part = half // 4
    out_copies = []
    for i in range(half - 2, -1, -1):
        j = depth - 1 - i
        ulo = V[i] * D[i] + M[i] * ulo
        uhi = V[j] * D[j] + M[j] * uhi
        O[i] = ulo * S[i]
        O[j] = uhi * S[j]
        if i % part == 0:
            for start in (i, j + 1 - part):
                planes = pl.ds(start, part)
                out_copies.append(
                    pltpu.make_async_copy(
                        O.at[planes], out_ref.at[planes], out_sem.at[len(out_copies)]
                    )
                )
                out_copies[-1].start()

    for copy, sends, _ in halos:
        pl.when(sends)(copy.wait_send)
    for i in range(n):
        pl.when(me != i)(gather_copy(i).wait_send)
    for i in range(n):
        pl.when(me != i)(answer_copy(i).wait_send)
    for copy in wide_coefs + wide_values:
        copy.wait_send()
    for copy in out_copies:
        copy.wait()


def shards(n, nw, x, zones, spray_coef):
    depth, rows, lanes = x.shape
    pz = depth // n
    f32 = jnp.float32
    vmem = pltpu.VMEM
    bz = max(pz, depth // 2)
    nb = depth // bz
    field = vmem((depth, rows, lanes), f32)
    blocks = vmem((nb, rows, bz, lanes), f32)
    padded = vmem((depth + 2, rows, lanes), f32)
    levels = vmem(((lanes - 1).bit_length(), nb, rows, bz, lanes), f32)
    edge = vmem((depth, lanes), f32)
    packed = vmem((bz, lanes), f32)
    dma = pltpu.SemaphoreType.DMA
    scratch = (
        [pltpu.SMEM(spray_coef.shape, f32)]
        + [field, vmem(zones.shape, zones.dtype), padded, padded]
        + [field, field]
        + [blocks] * 6
        + [levels, levels]
        + [blocks] * 4
        + [field] * 4
        + [vmem((nb, bz, lanes), f32)] * 2
        + [vmem((2, depth, lanes), f32), edge, edge, packed, packed, packed]
        + [
            vmem((n, 5 * pz, lanes), f32),
            vmem((n, 5 * pz, lanes), f32),
            vmem((n, 2 * pz, lanes), f32),
            vmem((n, 2 * pz, lanes), f32),
            vmem((nw, 2, bz, lanes), f32),
            vmem((nw, bz, lanes), f32),
        ]
        + [dma((3,)), dma((8,)), dma((4,)), dma((4,))]
        + [dma((n,))] * 4
        + [dma((nw,))] * 4
    )
    step = pl.pallas_call(
        functools.partial(kernel, n, nw),
        out_shape=jax.ShapeDtypeStruct(x.shape, f32),
        in_specs=[
            pl.BlockSpec(memory_space=pltpu.HBM),
            pl.BlockSpec(memory_space=pltpu.HBM),
            pl.BlockSpec(memory_space=pltpu.HBM),
        ],
        out_specs=pl.BlockSpec(memory_space=pltpu.HBM),
        scratch_shapes=scratch,
        compiler_params=pltpu.CompilerParams(
            collective_id=0, has_side_effects=True, vmem_limit_bytes=63 * 1024 * 1024
        ),
        cost_estimate=pl.CostEstimate(
            flops=20_000_000, bytes_accessed=1_000_000, transcendentals=100_000
        ),
        name="adi_step",
    )(x, zones, spray_coef)
    return x + step


def solution(mesh):
    spec = P(None, "cast", "width")
    body = functools.partial(shards, mesh.shape["cast"], mesh.shape["width"])
    return jax.shard_map(
        body, mesh=mesh, in_specs=(spec, spec, P()), out_specs=spec, check_vma=False
    )
```
